1024 devices in a mesh: dp: 64 (over y, z), feat: 16 (over x, core).
Axes of the slice: x: 8, y: 8, z: 8, core: 2. Of those that a mesh axis runs over, the one named last changes fastest.
Arguments:
- source_feat: bfloat16 [524288, 1024], P('dp', 'feat'), may hold values from -6 to 6
- weight: bfloat16 [1024, 512], P('feat'), may hold values from -0.1875 to 0.1875
- tile_index: int32 [1024, 8], P('dp'), may hold values from 0 to 63
- tile_count: int32 [1024], P('dp'), may hold values from 1 to 8, as said below
- tile_mask: int32 [1024, 8, 128, 128], P('dp'), may hold values 0 or 1
- cotangent: bfloat16 [131072, 512], P(('dp', 'feat')), may hold values from -6 to 6
Outputs:
- hidden: bfloat16 [131072, 512], P(('dp', 'feat'))
- weight_grad: float32 [1024, 512], P('feat')
The draws below stay inside these ranges and needn't reach their ends.
Inputs may be any that keep to these rules, and one draw needn't show every extreme that they name: `tile_count`: every target block has at least one live slot; in every dp group some blocks have all 8 slots live.
All inputs are finite; a program needn't handle non-finite values. No bound on the sum of `tile_mask` on one device may be relied on, other than what follows from the above.
Results may differ from the reference program's by a relative error of at most 0.0052.
Values may be sent and summed in bfloat16 or wider, within the bound.
A program may use at most 32 MiB of HBM per device.

```python
import jax
import jax.numpy as jnp
from jax import lax

F = 1024
H = 512
TILE = 128
MAXT = 8
TGT_DEV = 2048
SRC_DEV = 8192
TGT = 131072
SRC = 524288
NTB = 1024


def draw_tile_count(key, part):
    key = jax.random.fold_in(key, 11)
    count = jax.random.randint(key, (NTB,), 1, MAXT + 1)
    place = jnp.arange(NTB, dtype=jnp.int32)
    return jnp.where(place % 4 == 0, MAXT, count).astype(jnp.int32)


def set_ends(drawn, rng, low, top_value):
    longest = drawn.shape.index(max(drawn.shape))
    spots = []
    for shift in (0, 1):
        where = [jax.random.randint(jax.random.fold_in(rng, axis), (), 0, length) for axis, length in enumerate(drawn.shape)]
        where[longest] = (where[longest] + shift) % drawn.shape[longest]
        spots.append(tuple(where))
    return drawn.at[spots[0]].set(low).at[spots[1]].set(top_value)


def block_scale(stream_key, dims, cuts, low, high):
    gain, own = 1.0, jax.random.fold_in(stream_key, 6)
    for position, shards_of in cuts:
        steps = jnp.exp(jax.random.uniform(jax.random.fold_in(own, position), (shards_of,), jnp.float32, low / len(cuts), high / len(cuts)))
        gain = gain * jnp.repeat(steps, dims[position] // shards_of).reshape([-1 if axis == position else 1 for axis in range(len(dims))])
    return gain


def gaussian(key, dims, deviation, reach, pieces=(), kind=jnp.bfloat16):
    result = deviation * jax.random.normal(key, dims, jnp.float32)
    if pieces:
        result = result * block_scale(key, dims, pieces, -0.22, 0.18)
    return jnp.clip(result, -reach, reach).astype(kind)


def setup_inputs(seed: int = 0) -> dict:
    seeds = jax.random.split(jax.random.key(seed), 7)
    return {
        "source_feat": gaussian(seeds[0], (SRC, F), 1.0, 6.0, ((0, 64), (1, 16))),
        "weight": gaussian(seeds[1], (F, H), F ** -0.5, 0.1875, ((0, 16),)),
        "tile_index": set_ends(jax.random.randint(seeds[2], (NTB, MAXT), 0, SRC_DEV // TILE), jax.random.fold_in(seeds[2], 1), 0, (SRC_DEV // TILE) - 1).astype(jnp.int32),
        "tile_count": draw_tile_count(jax.random.fold_in(seeds[6], 71), 0),
        "tile_mask": set_ends((jax.random.randint(seeds[4], (NTB, MAXT, TILE, TILE), 0, 24) < 1).astype(jnp.int32), jax.random.fold_in(seeds[4], 1), 0, 1),
        "cotangent": gaussian(seeds[5], (TGT, H), 1.0, 6.0, ((0, 1024),)),
    }


def reference(source_feat, weight, tile_index, tile_count, tile_mask, cotangent):
    nblk = TGT_DEV // TILE
    groups = TGT // TGT_DEV

    def one_group(g):
        feats = lax.dynamic_slice_in_dim(source_feat, g * SRC_DEV, SRC_DEV, 0)
        blocks = feats.reshape(SRC_DEV // TILE, TILE, F)
        index = lax.dynamic_slice_in_dim(tile_index, g * nblk, nblk, 0)
        count = lax.dynamic_slice_in_dim(tile_count, g * nblk, nblk, 0)
        masks = lax.dynamic_slice_in_dim(tile_mask, g * nblk, nblk, 0)
        slots = lax.broadcasted_iota(jnp.int32, (nblk, MAXT), 1)
        live = slots < count[:, None]
        links = jnp.where(live[:, :, None, None], masks, 0)
        degree = jnp.maximum(jnp.sum(links, axis=(1, 3)), 1).astype(jnp.float32)
        picked = jnp.take(blocks, index, axis=0).astype(jnp.float32)
        summed = jnp.einsum("bsij,bsjf->bif", links.astype(jnp.float32), picked)
        return (summed / degree[:, :, None]).reshape(TGT_DEV, F).astype(jnp.bfloat16)

    agg = lax.map(one_group, jnp.arange(groups, dtype=jnp.int32)).reshape(TGT, F)
    z = jnp.dot(agg, weight, preferred_element_type=jnp.float32)
    sig = jax.nn.sigmoid(z)
    hidden = (z * sig).astype(jnp.bfloat16)
    dz = (cotangent.astype(jnp.float32) * sig * (1.0 + z * (1.0 - sig))).astype(jnp.bfloat16)
    weight_grad = jnp.dot(agg.T, dz, preferred_element_type=jnp.float32)
    return hidden, weight_grad
```

```python
import functools

import jax
import jax.numpy as jnp
from jax import lax
from jax.experimental import pallas as pl
from jax.experimental.pallas import tpu as pltpu
from jax.sharding import PartitionSpec as P

MESH = pl.DeviceIdType.MESH
TILE = 128
AHEAD = 3


def kernel(
    nx, n, maxt, width, tix, tcnt, src, weight, mask, cot, hid_out, wg_out,
    src_v, srcx, mask_v, w_own, cot_own, cot_x, cot_t, w_ab, w_t, agg_send, agg_full,
    hid_buf, hid_rx, p1_send, p1_recv, p2_send, p2_recv, p3_send, p3_recv, res, wg_acc,
    src_sem, mask_sem, w_sem, cot_sem, cx_send, cx_recv, w1_send, w1_recv, w2_send, w2_recv,
    a_send, a_recv, f_send, f_recv, p1_ss, p1_rs, p2_ss, p2_rs, p3_ss, p3_rs, p4_ss, p4_rs, h_send, h_recv,
):
    dp = lax.axis_index("dp")
    feat = lax.axis_index("feat")
    y, z = lax.div(dp, n), lax.rem(dp, n)
    x, c = lax.div(feat, 2), lax.rem(feat, 2)
    half = n // 2
    rows = TILE // n
    place = (y, z)
    f32, bf16 = jnp.float32, jnp.bfloat16

    def at(ab, i):
        return i * n + z if ab == 0 else y * n + i

    def remote(source, target, ssem, rsem, where):
        return pltpu.make_async_remote_copy(
            src_ref=source, dst_ref=target, send_sem=ssem, recv_sem=rsem, device_id=where, device_id_type=MESH
        )

    def each(count, body):
        def step(i, carry):
            body(i)
            return carry

        lax.fori_loop(0, count, step, 0)

    def served(step):
        off = jnp.where(lax.rem(step, 2) == 1, lax.div(nx - 1 - step, 2), nx // 2 + lax.div(step, 2))
        return off

    def mask_copy(step):
        chip = lax.rem(x + served(step), nx)
        return pltpu.make_async_copy(mask.at[pl.ds(2 * chip, 2)], mask_v.at[step], mask_sem.at[step])

    get_src = pltpu.make_async_copy(src, src_v, src_sem)
    get_src.start()
    get_w = pltpu.make_async_copy(weight, w_own, w_sem)
    get_w.start()
    get_cot = pltpu.make_async_copy(cot, cot_own, cot_sem)
    get_cot.start()
    for k in range(min(AHEAD, nx)):
        mask_copy(jnp.int32(k)).start()

    barrier = pltpu.get_barrier_semaphore()

    def greet(where):
        pl.semaphore_signal(barrier, inc=1, device_id=where, device_id_type=MESH)

    def greet_feat(i):
        greet((dp, lax.rem(feat + 1 + i, 2 * nx)))

    def greet_axes(i):
        for ab in (0, 1):
            for core in (0, 1):
                greet((at(ab, lax.rem(place[ab] + 1 + i, n)), 2 * x + core))

    each(2 * nx - 1, greet_feat)
    each(n - 1, greet_axes)

    get_src.wait()
    lane = lax.broadcasted_iota(jnp.int32, (TILE, TILE - width), 1)
    tail = jnp.where(lane == 0, 1.0, 0.0).astype(bf16)

    def widen(i):
        srcx[i] = jnp.concatenate([src_v[i], tail], axis=1)

    each(src_v.shape[0], widen)
    get_w.wait()
    get_cot.wait()

    def w1_copy(ab, to_x, to_c):
        return remote(
            w_own.at[lax.rem(place[ab], half), :, pl.ds(2 * TILE * to_c + TILE * ab, TILE)],
            w_ab.at[ab, x, place[ab]],
            w1_send.at[ab, to_c, to_x],
            w1_recv.at[ab, x],
            (dp, 2 * to_x + to_c),
        )

    def w1_self(ab, from_x):
        return jnp.logical_and(from_x == x, c == lax.div(place[ab], half))

    def send_w1():
        for ab in (0, 1):
            @pl.when(c == lax.div(place[ab], half))
            def _():
                for to_c in (0, 1):
                    def go(to_x):
                        own = jnp.logical_and(to_x == x, to_c == c)

                        @pl.when(jnp.logical_not(own))
                        def _():
                            w1_copy(ab, to_x, to_c).start()

                        @pl.when(own)
                        def _():
                            w_ab[ab, x, place[ab]] = w_own[
                                lax.rem(place[ab], half), :, 2 * TILE * to_c + TILE * ab : 2 * TILE * to_c + TILE * (ab + 1)
                            ]

                    each(nx, go)

    def w1_wait_recv(ab, from_x):
        remote(
            w_own.at[0, :, pl.ds(0, TILE)],
            w_ab.at[ab, from_x, place[ab]],
            w1_send.at[ab, 0, 0],
            w1_recv.at[ab, from_x],
            (dp, feat),
        ).wait_recv()

    def w2_copy(ab, i):
        return remote(
            w_ab.at[ab, :, place[ab]],
            w_ab.at[ab, :, place[ab]],
            w2_send.at[ab, i],
            w2_recv.at[ab, place[ab]],
            (at(ab, i), feat),
        )

    def w2_wait_recv(ab, i):
        remote(
            w_ab.at[ab, :, place[ab]], w_ab.at[ab, :, i], w2_send.at[ab, i], w2_recv.at[ab, i], (at(ab, i), feat)
        ).wait_recv()

    def others(ab, body):
        def go(i):
            body(lax.rem(place[ab] + 1 + i, n))

        each(n - 1, go)

    def send_w2():
        for ab in (0, 1):
            def arrive(from_x):
                @pl.when(jnp.logical_not(w1_self(ab, from_x)))
                def _():
                    w1_wait_recv(ab, from_x)

            each(nx, arrive)
            others(ab, lambda i: w2_copy(ab, i).start())

    def cot_copy():
        return remote(
            cot_own.at[:, pl.ds(pl.multiple_of((1 - c) * 2 * TILE, TILE), 2 * TILE)],
            cot_x.at[c],
            cx_send,
            cx_recv,
            (dp, 2 * x + 1 - c),
        )

    def a_copy(step, to_x):
        return remote(agg_send.at[step], agg_full.at[2 * x + c], a_send.at[step], a_recv.at[x], (dp, 2 * to_x + c))

    def a_wait_recv(from_x):
        remote(
            agg_send.at[0], agg_full.at[2 * from_x + c], a_send.at[0], a_recv.at[from_x], (dp, feat)
        ).wait_recv()

    def f_copy(from_x):
        return remote(
            agg_full.at[2 * from_x + c],
            agg_full.at[2 * from_x + c],
            f_send.at[from_x],
            f_recv.at[from_x],
            (dp, 2 * x + 1 - c),
        )

    def f_wait_recv(from_x):
        remote(
            agg_full.at[2 * from_x + c],
            agg_full.at[2 * from_x + 1 - c],
            f_send.at[from_x],
            f_recv.at[from_x],
            (dp, 2 * x + 1 - c),
        ).wait_recv()

    def forward(step):
        from_x = lax.rem(x + nx - served(step), nx)
        a_wait_recv(from_x)
        f_copy(from_x).start()

    def aggregate(step, k, chip):
        b = 2 * chip + k
        count = tcnt[b]
        links = [mask_v[step, k, s].astype(f32).astype(bf16) for s in range(maxt)]
        picks = [jnp.where(s < count, srcx[tix[b, s]], jnp.zeros((), bf16)) for s in range(maxt)]
        total = jnp.dot(
            jnp.concatenate(links, axis=1), jnp.concatenate(picks, axis=0), preferred_element_type=f32
        )
        total = total.T
        return (total[:width] / jnp.maximum(total[width : width + 1], 1.0)).astype(bf16)

    def chip_step(step):
        chip = lax.rem(x + served(step), nx)
        mask_copy(step).wait()

        @pl.when(step + AHEAD < nx)
        def _():
            mask_copy(step + AHEAD).start()

        for k in (0, 1):
            agg_send[step, :, k * TILE : (k + 1) * TILE] = aggregate(step, k, chip)

        @pl.when(step == 0)
        def _():
            pl.semaphore_wait(barrier, 2 * nx - 1 + 4 * (n - 1))
            send_w1()
            cot_copy().start()

        @pl.when(step == min(2, nx - 1))
        def _():
            send_w2()

        @pl.when(step < nx - 1)
        def _():
            a_copy(step, chip).start()

        @pl.when(step >= 2)
        def _():
            forward(step - 2)

    each(nx, chip_step)
    agg_full[2 * x + c] = agg_send[nx - 1]
    f_copy(x).start()
    if nx >= 2:
        forward(jnp.int32(nx - 2))

    cot_x[c] = cot_own[:, pl.ds(pl.multiple_of(c * 2 * TILE, TILE), 2 * TILE)]
    remote(cot_own.at[:, pl.ds(0, 2 * TILE)], cot_x.at[1 - c], cx_send, cx_recv, (dp, 2 * x + 1 - c)).wait_recv()
    for k in (0, 1):
        cot_t[:, k * TILE : (k + 1) * TILE] = cot_x[k].astype(f32).T
    for ab in (0, 1):
        others(ab, functools.partial(w2_wait_recv, ab))
        w_t[ab * TILE : (ab + 1) * TILE, :] = w_ab[ab].reshape(nx * TILE, TILE).T

    each(nx, f_wait_recv)
    agg = agg_full[...].reshape(nx * TILE, 2 * TILE)
    zt = jnp.dot(w_t[...], agg, preferred_element_type=f32)
    sig = jax.nn.sigmoid(zt)
    hid_t = zt * sig
    dzt = (cot_t[...] * sig * (1.0 + zt * (1.0 - sig))).astype(bf16)
    part = lax.dot_general(agg, dzt, (((1,), (1,)), ((), ())), preferred_element_type=f32).astype(bf16)
    for ab in (0, 1):
        block = part[:, ab * TILE : (ab + 1) * TILE].reshape(nx, n, rows, TILE)
        for i in range(n):
            p1_send[ab, i] = block[:, i]

    def p1_copy(ab, i):
        return remote(
            p1_send.at[ab, i], p1_recv.at[ab, place[ab]], p1_ss.at[ab, i], p1_rs.at[ab, place[ab]], (at(ab, i), feat)
        )

    def p1_wait(ab, i):
        remote(
            p1_send.at[ab, i], p1_recv.at[ab, i], p1_ss.at[ab, i], p1_rs.at[ab, i], (at(ab, i), feat)
        ).wait_recv()

    for ab in (0, 1):
        others(ab, lambda i: p1_copy(ab, i).start())

    for k in (0, 1):
        hid_buf[k] = hid_t[:, k * TILE : (k + 1) * TILE].T.astype(bf16)
    hid_copy = remote(hid_buf.at[1 - c], hid_rx, h_send, h_recv, (dp, 2 * x + 1 - c))
    hid_copy.start()
    hid_out[:, pl.ds(pl.multiple_of(c * 2 * TILE, TILE), 2 * TILE)] = hid_buf[c]

    for ab in (0, 1):
        p1_recv[ab, place[ab]] = p1_send[ab, place[ab]]
        others(ab, functools.partial(p1_wait, ab))
        p2_send[:, ab] = jnp.sum(p1_recv[ab].astype(f32), axis=0).astype(bf16)

    def p2_copy(i):
        return remote(p2_send.at[i], p2_recv.at[x], p2_ss.at[i], p2_rs.at[x], (dp, 2 * i + c))

    def p2_wait(i):
        remote(p2_send.at[i], p2_recv.at[i], p2_ss.at[i], p2_rs.at[i], (dp, 2 * i + c)).wait_recv()

    def others_x(body):
        each(nx - 1, lambda i: body(lax.rem(x + 1 + i, nx)))

    others_x(lambda i: p2_copy(i).start())
    p2_recv[x] = p2_send[x]
    others_x(p2_wait)
    p3_send[...] = jnp.sum(p2_recv[...].astype(f32), axis=0)

    def p3_copy(ab, i):
        return remote(
            p3_send.at[ab], p3_recv.at[ab, place[1 - ab]], p3_ss.at[ab, i], p3_rs.at[ab, place[1 - ab]], (at(1 - ab, i), feat)
        )

    def p3_wait(ab, i):
        remote(
            p3_send.at[ab], p3_recv.at[ab, i], p3_ss.at[ab, i], p3_rs.at[ab, i], (at(1 - ab, i), feat)
        ).wait_recv()

    for ab in (0, 1):
        others(1 - ab, lambda i: p3_copy(ab, i).start())
    for ab in (0, 1):
        p3_recv[ab, place[1 - ab]] = p3_send[ab]
        others(1 - ab, functools.partial(p3_wait, ab))
        res[ab] = jnp.sum(p3_recv[ab], axis=0)

    def wg_at(ab, chunk, core):
        return wg_acc.at[chunk, :, pl.ds(pl.multiple_of(2 * TILE * core + TILE * ab, TILE), TILE)]

    def p4_copy(ab, i):
        return remote(
            res.at[ab],
            wg_at(ab, lax.rem(place[ab], half), c),
            p4_ss.at[ab, i],
            p4_rs.at[ab, lax.rem(place[ab], half), c],
            (at(ab, i), 2 * x + lax.div(place[ab], half)),
        )

    def p4_self(ab, i):
        return jnp.logical_and(i == place[ab], c == lax.div(place[ab], half))

    def p4_go(ab, start):
        def go(i):
            @pl.when(jnp.logical_not(p4_self(ab, i)))
            def _():
                copy = p4_copy(ab, i)
                copy.start() if start else copy.wait_send()

        each(n, go)

    for ab in (0, 1):
        p4_go(ab, True)

        @pl.when(c == lax.div(place[ab], half))
        def _():
            wg_acc[lax.rem(place[ab], half), :, pl.ds(pl.multiple_of(2 * TILE * c + TILE * ab, TILE), TILE)] = res[ab]

    hid_copy.wait()
    hid_out[:, pl.ds(pl.multiple_of((1 - c) * 2 * TILE, TILE), 2 * TILE)] = hid_rx[...]

    for ab in (0, 1):
        @pl.when(c == lax.div(place[ab], half))
        def _():
            for to_c in (0, 1):
                def gone(to_x):
                    @pl.when(jnp.logical_not(jnp.logical_and(to_x == x, to_c == c)))
                    def _():
                        w1_copy(ab, to_x, to_c).wait_send()

                each(nx, gone)
        others(ab, lambda i: w2_copy(ab, i).wait_send())
        others(ab, lambda i: p1_copy(ab, i).wait_send())
        others(1 - ab, lambda i: p3_copy(ab, i).wait_send())
        p4_go(ab, False)
    cot_copy().wait_send()
    each(nx - 1, lambda i: a_copy(i, jnp.int32(0)).wait_send())
    each(nx, lambda i: f_copy(i).wait_send())
    others_x(lambda i: p2_copy(i).wait_send())

    for ab in (0, 1):
        for core in (0, 1):
            def landed(chunk):
                own = jnp.logical_and(c == core, c * half + chunk == place[ab])

                @pl.when(jnp.logical_not(own))
                def _():
                    remote(
                        res.at[ab], wg_at(ab, chunk, core), p4_ss.at[ab, 0], p4_rs.at[ab, chunk, core], (dp, feat)
                    ).wait_recv()

            each(half, landed)
    wg_out[...] = wg_acc[...].reshape(wg_out.shape)


def solution(mesh):
    nx = mesh.shape["feat"] // 2
    n = round(mesh.shape["dp"] ** 0.5)

    def shards(source_feat, weight, tile_index, tile_count, tile_mask, cotangent):
        nblk, maxt, tile, _ = tile_mask.shape
        width = source_feat.shape[1]
        hid = weight.shape[1]
        rows = TILE // n
        half = n // 2
        bf16, f32 = jnp.bfloat16, jnp.float32
        dma = lambda *shape: pltpu.SemaphoreType.DMA(shape)
        vm = pltpu.VMEM
        nsrc = source_feat.shape[0] // tile
        anyspec = pl.BlockSpec(memory_space=pl.ANY)
        smem = pl.BlockSpec(memory_space=pltpu.SMEM)
        vmem = pl.BlockSpec(memory_space=pltpu.VMEM)
        hidden, weight_grad = pl.pallas_call(
            functools.partial(kernel, nx, n, maxt, width),
            out_shape=(
                jax.ShapeDtypeStruct((tile, hid), bf16),
                jax.ShapeDtypeStruct((width, hid), f32),
            ),
            in_specs=[smem, smem, anyspec, anyspec, anyspec, anyspec],
            out_specs=(vmem, vmem),
            scratch_shapes=[
                vm((nsrc, tile, width), bf16),
                vm((nsrc, tile, TILE), bf16),
                vm((nx, 2, maxt, tile, tile), jnp.int32),
                vm((half, rows, hid), bf16),
                vm((tile, hid), bf16),
                vm((2, tile, 2 * TILE), bf16),
                vm((2 * TILE, 2 * tile), f32),
                vm((2, nx, n, rows, TILE), bf16),
                vm((2 * TILE, nx * TILE), bf16),
                vm((nx, width, 2 * tile), bf16),
                vm((2 * nx, width, 2 * tile), bf16),
                vm((2, tile, 2 * TILE), bf16),
                vm((tile, 2 * TILE), bf16),
                vm((2, n, nx, rows, TILE), bf16),
                vm((2, n, nx, rows, TILE), bf16),
                vm((nx, 2, rows, TILE), bf16),
                vm((nx, 2, rows, TILE), bf16),
                vm((2, rows, TILE), f32),
                vm((2, n, rows, TILE), f32),
                vm((2, rows, TILE), f32),
                vm((half, rows, hid), f32),
                dma(), dma(nx), dma(), dma(),
                dma(), dma(),
                dma(2, 2, nx), dma(2, nx),
                dma(2, n), dma(2, n),
                dma(nx), dma(nx),
                dma(nx), dma(nx),
                dma(2, n), dma(2, n),
                dma(nx), dma(nx),
                dma(2, n), dma(2, n),
                dma(2, n), dma(2, half, 2),
                dma(), dma(),
            ],
            compiler_params=pltpu.CompilerParams(
                collective_id=0, has_side_effects=True, vmem_limit_bytes=40 * 1024 * 1024
            ),
        )(
            tile_index,
            tile_count,
            source_feat.reshape(nsrc, tile, width),
            weight.reshape(half, rows, hid),
            tile_mask,
            cotangent,
        )
        return hidden, weight_grad

    in_specs = (
        P("dp", "feat"),
        P("feat", None),
        P("dp", None),
        P("dp"),
        P("dp", None, None, None),
        P(("dp", "feat"), None),
    )
    out_specs = (P(("dp", "feat"), None), P("feat", None))
    return jax.shard_map(shards, mesh=mesh, in_specs=in_specs, out_specs=out_specs, check_vma=False)
```

```python
import functools

import jax
import jax.numpy as jnp
from jax import lax
from jax.experimental import pallas as pl
from jax.experimental.pallas import tpu as pltpu
from jax.sharding import PartitionSpec as P

MESH = pl.DeviceIdType.MESH
TILE = 128


def around(n):
    return sorted(range(1, n), key=lambda k: (-min(k, n - k), -k))


def slots(n):
    return [0] + around(n)[::-1]


def kernel(
    nx, n, maxt, width, tix_h, tcnt_h, src, weight, mask, cot, hid_out, wg_out,
    tix, tcnt, src_v, src_x, mask_v, w_own, cot_own, cot_x, cot_t, w_ab, w_t, agg_send, agg_full,
    hid_buf, hid_rx, p1_send, p1_recv, p2_send, p2_recv, p3_send, p3_recv, res, wg_acc,
    ix_sem, src_sem, mask_sem, w_sem, cot_sem, cx_send, cx_recv, wd_send, wd_recv, w1_send, w1_recv, w2_send, w2_recv,
    a_send, a_recv, f_send, f_recv, p1_ss, p1_rs, p2_ss, p2_rs, p3_ss, p3_rs, p4_ss, p4_rs, h_send, h_recv,
):
    dp = lax.axis_index("dp")
    feat = lax.axis_index("feat")
    y, z = lax.div(dp, n), lax.rem(dp, n)
    x, c = lax.div(feat, 2), lax.rem(feat, 2)
    half = n // 2
    rows = TILE // n
    rel = slots(nx)
    near = min(3, nx)
    far = [(a, b) for a, b in ((near, min(near + 2, nx)), (near + 2, nx)) if a < b]
    place = (y, z)
    f32, bf16 = jnp.float32, jnp.bfloat16

    def at(ab, i):
        return i * n + z if ab == 0 else y * n + i

    def remote(source, target, ssem, rsem, where):
        return pltpu.make_async_remote_copy(
            src_ref=source, dst_ref=target, send_sem=ssem, recv_sem=rsem, device_id=where, device_id_type=MESH
        )

    def each(count, body):
        def step(i, carry):
            body(i)
            return carry

        lax.fori_loop(0, count, step, 0)

    def served(step):
        off = jnp.where(lax.rem(step, 2) == 1, lax.div(nx - 1 - step, 2), nx // 2 + lax.div(step, 2))
        return off

    def mask_copy(step):
        chip = lax.rem(x + served(step), nx)
        return pltpu.make_async_copy(mask.at[pl.ds(2 * chip, 2)], mask_v.at[step], mask_sem.at[step])

    barrier = pltpu.get_barrier_semaphore()

    def greet(where):
        pl.semaphore_signal(barrier, inc=1, device_id=where, device_id_type=MESH)

    for off in around(nx):
        for core in (0, 1):
            greet((dp, 2 * lax.rem(x + off, nx) + core))
    for off in around(n):
        for ab in (0, 1):
            for core in (0, 1):
                greet((at(ab, lax.rem(place[ab] + off, n)), 2 * x + core))
    greet((dp, 2 * x + 1 - c))

    get_ix = [pltpu.make_async_copy(a, b, ix_sem.at[i]) for i, (a, b) in enumerate(((tix_h, tix), (tcnt_h, tcnt)))]
    for copy in get_ix:
        copy.start()
    get_src = pltpu.make_async_copy(src, src_v, src_sem)
    get_src.start()
    get_w = pltpu.make_async_copy(weight, w_own, w_sem)
    get_w.start()
    get_cot = pltpu.make_async_copy(cot, cot_own, cot_sem)
    get_cot.start()
    for k in range(nx):
        mask_copy(jnp.int32(k)).start()

    def w_part(ab, to_c):
        return pl.ds(pl.multiple_of(2 * TILE * to_c + TILE * ab, TILE), TILE)

    def chip_at(steps):
        return lax.rem(x + nx + steps, nx)

    def wd_copy(ab, slot, to_c):
        return remote(
            w_own.at[:, :, w_part(ab, to_c)],
            w_ab.at[ab, slot, pl.ds(half * c, half)],
            wd_send.at[ab, slot, to_c],
            wd_recv.at[ab, slot, c],
            (dp, 2 * chip_at(-rel[slot]) + to_c),
        )

    def wd_wait_recv(ab, slot, from_c):
        remote(
            w_own.at[:, :, pl.ds(0, TILE)],
            w_ab.at[ab, slot, pl.ds(half * from_c, half)],
            wd_send.at[ab, slot, 0],
            wd_recv.at[ab, slot, from_c],
            (dp, feat),
        ).wait_recv()

    def w1_copy(ab, slot, to_c):
        return remote(
            w_own.at[lax.rem(place[ab], half), :, w_part(ab, to_c)],
            w_ab.at[ab, slot, place[ab]],
            w1_send.at[ab, slot, to_c],
            w1_recv.at[ab, slot],
            (dp, 2 * chip_at(-rel[slot]) + to_c),
        )

    def w1_all(body):
        for ab in (0, 1):
            @pl.when(c == lax.div(place[ab], half))
            def _():
                for slot in reversed(range(near, nx)):
                    for to_c in (0, 1):
                        body(w1_copy(ab, slot, to_c))

    def wd_all(body):
        for ab in (0, 1):
            body(wd_copy(ab, 0, 1 - c))
            for slot in range(1, near):
                for to_c in (0, 1):
                    body(wd_copy(ab, slot, to_c))

    def w2_copy(ab, group, i):
        piece = w_ab.at[ab, far[group][0] : far[group][1], place[ab]]
        return remote(piece, piece, w2_send.at[ab, group, i], w2_recv.at[ab, group, place[ab]], (at(ab, i), feat))

    def w2_wait_recv(ab, group, i):
        remote(
            w_ab.at[ab, far[group][0] : far[group][1], place[ab]],
            w_ab.at[ab, far[group][0] : far[group][1], i],
            w2_send.at[ab, group, i],
            w2_recv.at[ab, group, i],
            (at(ab, i), feat),
        ).wait_recv()

    def others(ab, body):
        for off in around(n):
            body(lax.rem(place[ab] + off, n))

    def send_w2(group):
        for ab in (0, 1):
            for slot in range(*far[group]):
                remote(
                    w_own.at[0, :, pl.ds(0, TILE)],
                    w_ab.at[ab, slot, place[ab]],
                    w1_send.at[ab, slot, 0],
                    w1_recv.at[ab, slot],
                    (dp, feat),
                ).wait_recv()
            others(ab, lambda i, ab=ab: w2_copy(ab, group, i).start())

    def turn_w(first, last):
        for ab in (0, 1):
            for slot in range(first, last):
                w_t[ab * TILE : (ab + 1) * TILE, slot * TILE : (slot + 1) * TILE] = w_ab[ab, slot].reshape(TILE, TILE).T

    def cot_copy():
        return remote(
            cot_own.at[:, pl.ds(pl.multiple_of((1 - c) * 2 * TILE, TILE), 2 * TILE)],
            cot_x.at[c],
            cx_send,
            cx_recv,
            (dp, 2 * x + 1 - c),
        )

    def a_copy(step, to_x):
        slot = nx - 1 - step
        return remote(agg_send.at[step], agg_full.at[2 * slot + c], a_send.at[step], a_recv.at[slot], (dp, 2 * to_x + c))

    def f_copy(slot):
        return remote(
            agg_full.at[2 * slot + c],
            agg_full.at[2 * slot + c],
            f_send.at[slot],
            f_recv.at[slot],
            (dp, 2 * x + 1 - c),
        )

    def f_wait_recv(slot):
        remote(
            agg_full.at[2 * slot + c],
            agg_full.at[2 * slot + 1 - c],
            f_send.at[slot],
            f_recv.at[slot],
            (dp, 2 * x + 1 - c),
        ).wait_recv()

    def forward(step):
        slot = nx - 1 - step
        remote(agg_send.at[0], agg_full.at[2 * slot + c], a_send.at[0], a_recv.at[slot], (dp, feat)).wait_recv()
        f_copy(slot).start()

    def aggregate(step, k, chip):
        b = 2 * chip + k
        count = tcnt[0, b]
        links, picks = [], []
        for s in range(maxt):
            links.append(mask_v[step, k, s].astype(f32).astype(bf16))
            picks.append(jnp.where(s < count, src_x[tix[s, b]], jnp.zeros((), bf16)))
        total = lax.dot_general(
            jnp.concatenate(picks, axis=1),
            jnp.concatenate(links, axis=1),
            (((1,), (1,)), ((), ())),
            preferred_element_type=f32,
        )
        return (total[:width] / jnp.maximum(total[width : width + 1], 1.0)).astype(bf16)

    def chip_step(step):
        chip = lax.rem(x + served(step), nx)
        mask_copy(step).wait()
        for k in (0, 1):
            agg_send[step, :, k * TILE : (k + 1) * TILE] = aggregate(step, k, chip)

        @pl.when(step < nx - 1)
        def _():
            a_copy(step, chip).start()

    get_w.wait()
    pl.semaphore_wait(barrier, 2 * nx - 1 + 4 * (n - 1))
    w1_all(lambda copy: copy.start())
    wd_all(lambda copy: copy.start())
    get_cot.wait()
    cot_copy().start()
    for copy in get_ix:
        copy.wait()
    get_src.wait()
    ones = jnp.ones((16, TILE), bf16)
    for i in range(src_x.shape[0]):
        src_x[i] = jnp.concatenate([src_v[:, i * TILE : (i + 1) * TILE], ones], axis=0)
    each(nx, chip_step)
    agg_full[c] = agg_send[nx - 1]
    f_copy(0).start()

    for group in range(len(far)):
        send_w2(group)
    each(nx - 1, forward)

    cot_x[c] = cot_own[:, pl.ds(pl.multiple_of(c * 2 * TILE, TILE), 2 * TILE)]
    remote(cot_own.at[:, pl.ds(0, 2 * TILE)], cot_x.at[1 - c], cx_send, cx_recv, (dp, 2 * x + 1 - c)).wait_recv()
    for k in (0, 1):
        cot_t[:, k * TILE : (k + 1) * TILE] = cot_x[k].astype(f32).T
    for ab in (0, 1):
        w_ab[ab, 0, pl.ds(half * c, half)] = w_own[:, :, w_part(ab, c)]
        wd_wait_recv(ab, 0, 1 - c)
        for slot in range(1, near):
            for from_c in (0, 1):
                wd_wait_recv(ab, slot, from_c)
    turn_w(0, near)
    for group, (first, last) in enumerate(far):
        for ab in (0, 1):
            others(ab, functools.partial(w2_wait_recv, ab, group))
        turn_w(first, last)

    each(nx, f_wait_recv)
    agg = agg_full[...].reshape(nx * TILE, 2 * TILE)
    zt = jnp.dot(w_t[...], agg, preferred_element_type=f32)
    sig = jax.nn.sigmoid(zt)
    hid_t = zt * sig
    dzt = (cot_t[...] * sig * (1.0 + zt * (1.0 - sig))).astype(bf16)

    def p1_copy(ab, i):
        return remote(
            p1_send.at[ab, i], p1_recv.at[ab, place[ab]], p1_ss.at[ab, i], p1_rs.at[ab, place[ab]], (at(ab, i), feat)
        )

    def p1_wait(ab, i):
        remote(
            p1_send.at[ab, i], p1_recv.at[ab, i], p1_ss.at[ab, i], p1_rs.at[ab, i], (at(ab, i), feat)
        ).wait_recv()

    for ab in (0, 1):
        part = lax.dot_general(
            agg, dzt[ab * TILE : (ab + 1) * TILE], (((1,), (1,)), ((), ())), preferred_element_type=f32
        )
        block = part.astype(bf16).reshape(nx, n, rows, TILE)
        for i in range(n):
            p1_send[ab, i] = block[:, i]
        others(ab, lambda i, ab=ab: p1_copy(ab, i).start())

    for k in (0, 1):
        hid_buf[k] = hid_t[:, k * TILE : (k + 1) * TILE].T.astype(bf16)
    hid_copy = remote(hid_buf.at[1 - c], hid_rx, h_send, h_recv, (dp, 2 * x + 1 - c))
    hid_copy.start()
    hid_out[:, pl.ds(pl.multiple_of(c * 2 * TILE, TILE), 2 * TILE)] = hid_buf[c]

    for ab in (0, 1):
        p1_recv[ab, place[ab]] = p1_send[ab, place[ab]]
        others(ab, functools.partial(p1_wait, ab))
        p2_send[:, ab] = jnp.sum(p1_recv[ab].astype(f32), axis=0).astype(bf16)

    def p2_copy(slot):
        return remote(
            p2_send.at[slot], p2_recv.at[slot], p2_ss.at[slot], p2_rs.at[slot], (dp, 2 * chip_at(rel[slot]) + c)
        )

    for slot in reversed(range(1, nx)):
        p2_copy(slot).start()
    p2_recv[0] = p2_send[0]
    for slot in range(1, nx):
        p2_copy(slot).wait_recv()
    p3_send[...] = jnp.sum(p2_recv[...].astype(f32), axis=0)

    def p3_copy(ab, i):
        return remote(
            p3_send.at[ab], p3_recv.at[ab, place[1 - ab]], p3_ss.at[ab, i], p3_rs.at[ab, place[1 - ab]], (at(1 - ab, i), feat)
        )

    def p3_wait(ab, i):
        remote(
            p3_send.at[ab], p3_recv.at[ab, i], p3_ss.at[ab, i], p3_rs.at[ab, i], (at(1 - ab, i), feat)
        ).wait_recv()

    for ab in (0, 1):
        others(1 - ab, lambda i, ab=ab: p3_copy(ab, i).start())
    for ab in (0, 1):
        p3_recv[ab, place[1 - ab]] = p3_send[ab]
        others(1 - ab, functools.partial(p3_wait, ab))
        res[ab] = jnp.sum(p3_recv[ab], axis=0)

    def wg_at(ab, chunk, core):
        return wg_acc.at[chunk, :, pl.ds(pl.multiple_of(2 * TILE * core + TILE * ab, TILE), TILE)]

    def p4_copy(ab, i):
        return remote(
            res.at[ab],
            wg_at(ab, lax.rem(place[ab], half), c),
            p4_ss.at[ab, i],
            p4_rs.at[ab, lax.rem(place[ab], half), c],
            (at(ab, i), 2 * x + lax.div(place[ab], half)),
        )

    def p4_go(ab, start):
        def go(i):
            copy = p4_copy(ab, i)
            copy.start() if start else copy.wait_send()

        others(ab, go)

        @pl.when(c != lax.div(place[ab], half))
        def _():
            go(place[ab])

    for ab in (0, 1):
        p4_go(ab, True)

        @pl.when(c == lax.div(place[ab], half))
        def _():
            wg_acc[lax.rem(place[ab], half), :, pl.ds(pl.multiple_of(2 * TILE * c + TILE * ab, TILE), TILE)] = res[ab]

    hid_copy.wait()
    hid_out[:, pl.ds(pl.multiple_of((1 - c) * 2 * TILE, TILE), 2 * TILE)] = hid_rx[...]

    w1_all(lambda copy: copy.wait_send())
    wd_all(lambda copy: copy.wait_send())
    for ab in (0, 1):
        for group in range(len(far)):
            others(ab, lambda i: w2_copy(ab, group, i).wait_send())
        others(ab, lambda i: p1_copy(ab, i).wait_send())
        others(1 - ab, lambda i: p3_copy(ab, i).wait_send())
        p4_go(ab, False)
    cot_copy().wait_send()
    each(nx - 1, lambda i: a_copy(i, jnp.int32(0)).wait_send())
    each(nx, lambda i: f_copy(i).wait_send())
    for slot in range(1, nx):
        p2_copy(slot).wait_send()

    for ab in (0, 1):
        for core in (0, 1):
            def landed(chunk):
                own = jnp.logical_and(c == core, c * half + chunk == place[ab])

                @pl.when(jnp.logical_not(own))
                def _():
                    remote(
                        res.at[ab], wg_at(ab, chunk, core), p4_ss.at[ab, 0], p4_rs.at[ab, chunk, core], (dp, feat)
                    ).wait_recv()

            each(half, landed)
    wg_out[...] = wg_acc[...].reshape(wg_out.shape)


def solution(mesh):
    nx = mesh.shape["feat"] // 2
    n = round(mesh.shape["dp"] ** 0.5)

    def shards(source_feat, weight, tile_index, tile_count, tile_mask, cotangent):
        nblk, maxt, tile, _ = tile_mask.shape
        width = source_feat.shape[1]
        hid = weight.shape[1]
        rows = TILE // n
        half = n // 2
        bf16, f32 = jnp.bfloat16, jnp.float32
        dma = lambda *shape: pltpu.SemaphoreType.DMA(shape)
        vm = pltpu.VMEM
        hbm = pl.BlockSpec(memory_space=pltpu.HBM)
        vmem = pl.BlockSpec(memory_space=pltpu.VMEM)
        hidden, weight_grad = pl.pallas_call(
            functools.partial(kernel, nx, n, maxt, width),
            out_shape=(
                vm((tile, hid), bf16),
                vm((width, hid), f32),
            ),
            in_specs=[hbm] * 6,
            out_specs=(vmem, vmem),
            scratch_shapes=[
                pltpu.SMEM((maxt, nblk), jnp.int32),
                pltpu.SMEM((1, nblk), jnp.int32),
                vm((width, source_feat.shape[0]), bf16),
                vm((source_feat.shape[0] // tile, width + 16, tile), bf16),
                vm((nx, 2, maxt, tile, tile), jnp.int32),
                vm((half, rows, hid), bf16),
                vm((tile, hid), bf16),
                vm((2, tile, 2 * TILE), bf16),
                vm((2 * TILE, 2 * tile), f32),
                vm((2, nx, n, rows, TILE), bf16),
                vm((2 * TILE, nx * TILE), bf16),
                vm((nx, width, 2 * tile), bf16),
                vm((2 * nx, width, 2 * tile), bf16),
                vm((2, tile, 2 * TILE), bf16),
                vm((tile, 2 * TILE), bf16),
                vm((2, n, nx, rows, TILE), bf16),
                vm((2, n, nx, rows, TILE), bf16),
                vm((nx, 2, rows, TILE), bf16),
                vm((nx, 2, rows, TILE), bf16),
                vm((2, rows, TILE), f32),
                vm((2, n, rows, TILE), f32),
                vm((2, rows, TILE), f32),
                vm((half, rows, hid), f32),
                dma(2), dma(), dma(nx), dma(), dma(),
                dma(), dma(),
                dma(2, 3, 2), dma(2, 3, 2),
                dma(2, nx, 2), dma(2, nx),
                dma(2, 2, n), dma(2, 2, n),
                dma(nx), dma(nx),
                dma(nx), dma(nx),
                dma(2, n), dma(2, n),
                dma(nx), dma(nx),
                dma(2, n), dma(2, n),
                dma(2, n), dma(2, half, 2),
                dma(), dma(),
            ],
            compiler_params=pltpu.CompilerParams(
                collective_id=0, has_side_effects=True, vmem_limit_bytes=40 * 1024 * 1024
            ),
        )(
            *(
                pltpu.with_memory_space_constraint(a, pltpu.HBM)
                for a in (
                    tile_index.T,
                    tile_count.reshape(1, nblk),
                    source_feat.T,
                    weight.reshape(half, rows, hid),
                    tile_mask,
                    cotangent,
                )
            )
        )
        return hidden, weight_grad

    in_specs = (
        P("dp", "feat"),
        P("feat", None),
        P("dp", None),
        P("dp"),
        P("dp", None, None, None),
        P(("dp", "feat"), None),
    )
    out_specs = (P(("dp", "feat"), None), P("feat", None))
    return jax.shard_map(shards, mesh=mesh, in_specs=in_specs, out_specs=out_specs, check_vma=False)
```

```python
import functools

import jax
import jax.numpy as jnp
from jax import lax
from jax.experimental import pallas as pl
from jax.experimental.pallas import tpu as pltpu
from jax.sharding import PartitionSpec as P

MESH = pl.DeviceIdType.MESH
TILE = 128


def around(n):
    return sorted(range(1, n), key=lambda k: (-min(k, n - k), -k))


def slots(n):
    return [0] + around(n)[::-1]


def kernel(
    nx, n, maxt, width, tix_h, tcnt_h, src, weight, mask, cot, hid_out, wg_out,
    tix, tcnt, src_v, src_x, mask_v, w_own, cot_own, cot_x, cot_t, w_ab, w_t, agg_send, agg_full,
    hid_buf, hid_rx, p1x_send, p1x_recv, p1_send, p1_recv, p2x_send, p2x_recv, p2_send, p2_recv, p3_send, p3_recv, res, wg_acc,
    ix_sem, src_sem, mask_sem, w_sem, cot_sem, cx_send, cx_recv, wd_send, wd_recv, w1_send, w1_recv, w2_send, w2_recv,
    a_send, a_recv, f_send, f_recv, p1x_ss, p1x_rs, p1_ss, p1_rs, p2x_ss, p2x_rs, p2_ss, p2_rs, p3_ss, p3_rs, p4_ss, p4_rs, h_send, h_recv,
):
    dp = lax.axis_index("dp")
    feat = lax.axis_index("feat")
    y, z = lax.div(dp, n), lax.rem(dp, n)
    x, c = lax.div(feat, 2), lax.rem(feat, 2)
    half = n // 2
    rows = TILE // n
    rel = slots(nx)
    near = min(3, nx)
    far = [(a, b) for a, b in ((near, min(near + 2, nx)), (near + 2, nx)) if a < b]
    place = (y, z)
    f32, bf16 = jnp.float32, jnp.bfloat16

    def at(ab, i):
        return i * n + z if ab == 0 else y * n + i

    def remote(source, target, ssem, rsem, where):
        return pltpu.make_async_remote_copy(
            src_ref=source, dst_ref=target, send_sem=ssem, recv_sem=rsem, device_id=where, device_id_type=MESH
        )

    def arrived(ref, sem):
        remote(ref, ref, sem, sem, (dp, feat)).wait_recv()

    def left(ref, sem):
        remote(ref, ref, sem, sem, (dp, feat)).wait_send()

    def each(count, body):
        def step(i, carry):
            body(i)
            return carry

        lax.fori_loop(0, count, step, 0)

    def served(step):
        off = jnp.where(lax.rem(step, 2) == 1, lax.div(nx - 1 - step, 2), nx // 2 + lax.div(step, 2))
        return off

    def mask_copy(step):
        chip = lax.rem(x + served(step), nx)
        return pltpu.make_async_copy(mask.at[pl.ds(2 * chip, 2)], mask_v.at[step], mask_sem.at[step])

    barrier = pltpu.get_barrier_semaphore()

    def greet(where):
        pl.semaphore_signal(barrier, inc=1, device_id=where, device_id_type=MESH)

    for off in around(nx):
        for core in (0, 1):
            greet((dp, 2 * lax.rem(x + off, nx) + core))
    for off in around(n):
        for ab in (0, 1):
            for core in (0, 1):
                greet((at(ab, lax.rem(place[ab] + off, n)), 2 * x + core))
    greet((dp, 2 * x + 1 - c))

    get_ix = [pltpu.make_async_copy(a, b, ix_sem.at[i]) for i, (a, b) in enumerate(((tix_h, tix), (tcnt_h, tcnt)))]
    for copy in get_ix:
        copy.start()
    get_src = pltpu.make_async_copy(src, src_v, src_sem)
    get_src.start()
    get_w = pltpu.make_async_copy(weight, w_own, w_sem)
    get_w.start()
    get_cot = pltpu.make_async_copy(cot, cot_own, cot_sem)
    get_cot.start()
    for k in range(nx):
        mask_copy(jnp.int32(k)).start()

    def w_part(ab, to_c):
        return pl.ds(pl.multiple_of(2 * TILE * to_c + TILE * ab, TILE), TILE)

    def chip_at(steps):
        return lax.rem(x + nx + steps, nx)

    def wd_copy(ab, slot, to_c):
        return remote(
            w_own.at[:, :, w_part(ab, to_c)],
            w_ab.at[ab, slot, pl.ds(half * c, half)],
            wd_send.at[min(slot, 1)],
            wd_recv.at[min(slot, 1)],
            (dp, 2 * chip_at(-rel[slot]) + to_c),
        )

    def w1_copy(ab, slot, to_c):
        return remote(
            w_own.at[lax.rem(place[ab], half), :, w_part(ab, to_c)],
            w_ab.at[ab, slot, place[ab]],
            w1_send.at[ab],
            w1_recv.at[ab, [k for k, (a, b) in enumerate(far) if a <= slot < b][0]],
            (dp, 2 * chip_at(-rel[slot]) + to_c),
        )

    def sends_w1(ab):
        return c == lax.div(place[ab], half)

    def w2_copy(ab, group, i):
        piece = w_ab.at[ab, far[group][0] : far[group][1], place[ab]]
        return remote(piece, piece, w2_send.at[ab, group], w2_recv.at[ab, group], (at(ab, i), feat))

    def others(ab, body):
        for off in around(n):
            body(lax.rem(place[ab] + off, n))

    def send_w2(group):
        for ab in (0, 1):
            arrived(w_ab.at[ab, far[group][0] : far[group][1], place[ab]], w1_recv.at[ab, group])
            others(ab, lambda i, ab=ab: w2_copy(ab, group, i).start())

    def turn_w(first, last):
        for ab in (0, 1):
            for slot in range(first, last):
                w_t[ab * TILE : (ab + 1) * TILE, slot * TILE : (slot + 1) * TILE] = w_ab[ab, slot].reshape(TILE, TILE).T

    def cot_copy():
        return remote(
            cot_own.at[:, pl.ds(pl.multiple_of((1 - c) * 2 * TILE, TILE), 2 * TILE)],
            cot_x.at[c],
            cx_send,
            cx_recv,
            (dp, 2 * x + 1 - c),
        )

    def a_copy(step, to_x):
        slot = nx - 1 - step
        return remote(agg_send.at[step], agg_full.at[slot, c], a_send, a_recv.at[slot], (dp, 2 * to_x + c))

    def f_copy(slot):
        return remote(agg_full.at[slot, c], agg_full.at[slot, c], f_send, f_recv, (dp, 2 * x + 1 - c))

    def forward(step):
        slot = nx - 1 - step
        arrived(agg_full.at[slot, c], a_recv.at[slot])
        f_copy(slot).start()

    def aggregate(step, k, chip):
        b = 2 * chip + k
        count = tcnt[0, b]
        links, picks = [], []
        for s in range(maxt):
            links.append(mask_v[step, k, s].astype(f32).astype(bf16))
            picks.append(jnp.where(s < count, src_x[tix[s, b]], jnp.zeros((), bf16)))
        total = lax.dot_general(
            jnp.concatenate(picks, axis=1),
            jnp.concatenate(links, axis=1),
            (((1,), (1,)), ((), ())),
            preferred_element_type=f32,
        )
        return (total[:width] / jnp.maximum(total[width : width + 1], 1.0)).astype(bf16)

    def chip_step(step):
        chip = lax.rem(x + served(step), nx)
        mask_copy(step).wait()
        for k in (0, 1):
            agg_send[step, :, k * TILE : (k + 1) * TILE] = aggregate(step, k, chip)

        @pl.when(step < nx - 1)
        def _():
            a_copy(step, chip).start()

    get_w.wait()
    pl.semaphore_wait(barrier, 2 * nx - 1 + 4 * (n - 1))
    for ab in (0, 1):
        @pl.when(sends_w1(ab))
        def _():
            for slot in reversed(range(near, nx)):
                for to_c in (0, 1):
                    w1_copy(ab, slot, to_c).start()
    for slot in range(1, near):
        for ab in (0, 1):
            for to_c in (0, 1):
                wd_copy(ab, slot, to_c).start()
    for ab in (0, 1):
        wd_copy(ab, 0, 1 - c).start()
    get_cot.wait()
    cot_copy().start()
    for copy in get_ix:
        copy.wait()
    get_src.wait()
    ones = jnp.ones((16, TILE), bf16)
    for i in range(src_x.shape[0]):
        src_x[i] = jnp.concatenate([src_v[:, i * TILE : (i + 1) * TILE], ones], axis=0)
    each(nx, chip_step)
    agg_full[0, c] = agg_send[nx - 1]
    f_copy(0).start()

    for group in range(len(far)):
        send_w2(group)
    each(nx - 1, forward)

    cot_x[c] = cot_own[:, pl.ds(pl.multiple_of(c * 2 * TILE, TILE), 2 * TILE)]
    arrived(cot_x.at[1 - c], cx_recv)
    for k in (0, 1):
        cot_t[:, k * TILE : (k + 1) * TILE] = cot_x[k].astype(f32).T
    for ab in (0, 1):
        w_ab[ab, 0, pl.ds(half * c, half)] = w_own[:, :, w_part(ab, c)]
    arrived(w_ab.at[:, 0, pl.ds(half * (1 - c), half)], wd_recv.at[0])
    arrived(w_ab.at[:, 1:near], wd_recv.at[1])
    turn_w(0, near)
    for group, (first, last) in enumerate(far):
        for ab in (0, 1):
            arrived(w_ab.at[ab, first:last, 0 : n - 1], w2_recv.at[ab, group])
        turn_w(first, last)

    arrived(agg_full.at[:, 1 - c], f_recv)
    agg = agg_full[...].reshape(nx * TILE, 2 * TILE)
    zt = jnp.dot(w_t[...], agg, preferred_element_type=f32)
    sig = jax.nn.sigmoid(zt)
    hid_t = zt * sig
    dzt = (cot_t[...] * sig * (1.0 + zt * (1.0 - sig))).astype(bf16)

    turn = (0, 1, c)
    late = 1 - c
    r = TILE // 2 // n

    def spot(axis):
        return y + axis * (z - y)

    def to(axis, i):
        return i * n + z + axis * (y * n + i - i * n - z)

    def p1_copy(k, i):
        return remote(
            p1_send.at[k, i], p1_recv.at[k, spot(turn[k])], p1_ss.at[k], p1_rs.at[k], (to(turn[k], i), feat)
        )

    def p2x_copy(i):
        return remote(p2x_send.at[i], p2x_recv.at[spot(late)], p2x_ss, p2x_rs, (to(late, i), feat))

    def along(axis, body):
        for off in around(n):
            body(lax.rem(spot(axis) + off, n))

    def slot_copy(send, recv, ssem, rsem, slot):
        return remote(send.at[slot], recv.at[slot], ssem, rsem, (dp, 2 * chip_at(rel[slot]) + c))

    p1x_copy = functools.partial(slot_copy, p1x_send, p1x_recv, p1x_ss, p1x_rs)
    p2_copy = functools.partial(slot_copy, p2_send, p2_recv, p2_ss, p2_rs)

    for ab in (0, 1):
        part = lax.dot_general(
            agg, dzt[ab * TILE : (ab + 1) * TILE], (((1,), (1,)), ((), ())), preferred_element_type=f32
        ).reshape(nx, 2, n, r, TILE)
        for h in (0, 1):
            if ab + h == 0:
                p1x_send[...] = part[:, h].reshape(nx, TILE // 2, TILE).astype(bf16)
            else:
                for i in range(n):
                    p1_send[2 * ab + h - 1, i] = part[:, h, i].reshape(nx // 2, 2 * r, TILE).astype(bf16)
    for step in range(max(n, nx) - 1):
        if step < n - 1:
            for k in range(3):
                p1_copy(k, lax.rem(spot(turn[k]) + around(n)[step], n)).start()
        if step < nx - 1:
            p1x_copy(nx - 1 - step).start()

    for k in (0, 1):
        hid_buf[k] = hid_t[:, k * TILE : (k + 1) * TILE].T.astype(bf16)
    hid_copy = remote(hid_buf.at[1 - c], hid_rx, h_send, h_recv, (dp, 2 * x + 1 - c))
    hid_copy.start()
    hid_out[:, pl.ds(pl.multiple_of(c * 2 * TILE, TILE), 2 * TILE)] = hid_buf[c]

    for ab in (0, 1):
        if far:
            @pl.when(sends_w1(ab))
            def _():
                left(w_ab.at[ab, near:nx, 0:2], w1_send.at[ab])
        for group, (first, last) in enumerate(far):
            left(w_ab.at[ab, first:last, 0 : n - 1], w2_send.at[ab, group])
    left(w_ab.at[0, 0], wd_send.at[0])
    left(w_ab.at[:, 1:near], wd_send.at[1])
    left(cot_x.at[0], cx_send)
    left(agg_send.at[0 : nx - 1], a_send)
    left(agg_full.at[:, c], f_send)

    p1x_recv[0] = p1x_send[0]
    arrived(p1x_recv.at[1:nx], p1x_rs)
    p2x_send[...] = jnp.sum(p1x_recv[...].astype(f32), axis=0).reshape(n, r, TILE)
    along(late, lambda i: p2x_copy(i).start())
    for k in range(3):
        p1_recv[k, spot(turn[k])] = p1_send[k, spot(turn[k])]
        arrived(p1_recv.at[k, 0 : n - 1], p1_rs.at[k])
        p2_send[:, k] = jnp.sum(p1_recv[k].astype(f32), axis=0).reshape(nx, r, TILE)
    for slot in reversed(range(1, nx)):
        p2_copy(slot).start()
    left(p1x_send.at[1:nx], p1x_ss)
    for k in range(3):
        left(p1_send.at[k, 0 : n - 1], p1_ss.at[k])
    p2x_recv[spot(late)] = p2x_send[spot(late)]
    arrived(p2x_recv.at[0 : n - 1], p2x_rs)
    group0 = jnp.sum(p2x_recv[...], axis=0)
    p2_recv[0] = p2_send[0]
    arrived(p2_recv.at[1:nx], p2_rs)
    groups = jnp.sum(p2_recv[...], axis=0)

    for ab in (0, 1):
        p3_send[ab] = jnp.concatenate([groups[ab], jnp.where(c == ab, groups[2], group0)], axis=0).astype(bf16)

    def p3_copy(ab, i):
        return remote(p3_send.at[ab], p3_recv.at[ab, place[1 - ab]], p3_ss.at[ab], p3_rs.at[ab], (at(1 - ab, i), feat))

    for off in around(n):
        for ab in (0, 1):
            p3_copy(ab, lax.rem(place[1 - ab] + off, n)).start()
    left(p2x_send.at[0 : n - 1], p2x_ss)
    left(p2_send.at[1:nx], p2_ss)
    for ab in (0, 1):
        p3_recv[ab, place[1 - ab]] = p3_send[ab]
        arrived(p3_recv.at[ab, 0 : n - 1], p3_rs.at[ab])
        res[ab] = jnp.sum(p3_recv[ab].astype(f32), axis=0).reshape(2, r, TILE)

    def owner(ab, k):
        if k == 0:
            return 1 - ab, ab
        third = 1 - (c - ab) * (c - ab)
        return third, third

    def p4_copy(ab, k, i, sem):
        h, columns = owner(ab, k)
        return remote(
            res.at[ab, k], wg_acc.at[4 * place[ab] + 2 * c + columns], p4_ss.at[sem], p4_rs, (at(ab, i), 2 * x + h)
        )

    for off in around(n):
        for ab in (0, 1):
            for k in (0, 1):
                p4_copy(ab, k, lax.rem(place[ab] + off, n), 0).start()
    for ab in (0, 1):
        for k in (0, 1):
            @pl.when(owner(ab, k)[0] != c)
            def _():
                p4_copy(ab, k, place[ab], 1).start()

            @pl.when(owner(ab, k)[0] == c)
            def _():
                wg_acc[4 * place[ab] + 2 * c + owner(ab, k)[1]] = res[ab, k]

    hid_copy.wait()
    hid_out[:, pl.ds(pl.multiple_of((1 - c) * 2 * TILE, TILE), 2 * TILE)] = hid_rx[...]

    for ab in (0, 1):
        left(p3_recv.at[ab, 0 : n - 1], p3_ss.at[ab])
    left(wg_acc.at[0 : 4 * (n - 1)], p4_ss.at[0])
    left(res.at[0], p4_ss.at[1])

    arrived(wg_acc.at[0 : 4 * n - 2], p4_rs)
    for i in range(n):
        for block in range(4):
            wg_out[i * r : (i + 1) * r, block * TILE : (block + 1) * TILE] = wg_acc[4 * i + block]


def solution(mesh):
    nx = mesh.shape["feat"] // 2
    n = round(mesh.shape["dp"] ** 0.5)

    def shards(source_feat, weight, tile_index, tile_count, tile_mask, cotangent):
        nblk, maxt, tile, _ = tile_mask.shape
        width = source_feat.shape[1]
        hid = weight.shape[1]
        rows = TILE // n
        half = n // 2
        bf16, f32 = jnp.bfloat16, jnp.float32
        dma = lambda *shape: pltpu.SemaphoreType.DMA(shape)
        vm = pltpu.VMEM
        hbm = pl.BlockSpec(memory_space=pltpu.HBM)
        vmem = pl.BlockSpec(memory_space=pltpu.VMEM)
        hidden, weight_grad = pl.pallas_call(
            functools.partial(kernel, nx, n, maxt, width),
            out_shape=(
                vm((tile, hid), bf16),
                vm((width, hid), f32),
            ),
            in_specs=[hbm] * 6,
            out_specs=(vmem, vmem),
            scratch_shapes=[
                pltpu.SMEM((maxt, nblk), jnp.int32),
                pltpu.SMEM((1, nblk), jnp.int32),
                vm((width, source_feat.shape[0]), bf16),
                vm((source_feat.shape[0] // tile, width + 16, tile), bf16),
                vm((nx, 2, maxt, tile, tile), jnp.int32),
                vm((half, rows, hid), bf16),
                vm((tile, hid), bf16),
                vm((2, tile, 2 * TILE), bf16),
                vm((2 * TILE, 2 * tile), f32),
                vm((2, nx, n, rows, TILE), bf16),
                vm((2 * TILE, nx * TILE), bf16),
                vm((nx, width, 2 * tile), bf16),
                vm((nx, 2, width, 2 * tile), bf16),
                vm((2, tile, 2 * TILE), bf16),
                vm((tile, 2 * TILE), bf16),
                vm((nx, TILE // 2, TILE), bf16),
                vm((nx, TILE // 2, TILE), bf16),
                vm((3, n, nx // 2, rows, TILE), bf16),
                vm((3, n, nx // 2, rows, TILE), bf16),
                vm((n, rows // 2, TILE), f32),
                vm((n, rows // 2, TILE), f32),
                vm((nx, 3, rows // 2, TILE), f32),
                vm((nx, 3, rows // 2, TILE), f32),
                vm((2, rows, TILE), bf16),
                vm((2, n, rows, TILE), bf16),
                vm((2, 2, rows // 2, TILE), f32),
                vm((4 * n, rows // 2, TILE), f32),
                dma(2), dma(), dma(nx), dma(), dma(),
                dma(), dma(),
                dma(2), dma(2),
                dma(2), dma(2, 2),
                dma(2, 2), dma(2, 2),
                dma(), dma(nx),
                dma(), dma(),
                dma(), dma(),
                dma(3), dma(3),
                dma(), dma(),
                dma(), dma(),
                dma(2), dma(2),
                dma(2), dma(),
                dma(), dma(),
            ],
            compiler_params=pltpu.CompilerParams(
                collective_id=0, has_side_effects=True, vmem_limit_bytes=40 * 1024 * 1024
            ),
        )(
            *(
                pltpu.with_memory_space_constraint(a, pltpu.HBM)
                for a in (
                    tile_index.T,
                    tile_count.reshape(1, nblk),
                    source_feat.T,
                    weight.reshape(half, rows, hid),
                    tile_mask,
                    cotangent,
                )
            )
        )
        return hidden, weight_grad

    in_specs = (
        P("dp", "feat"),
        P("feat", None),
        P("dp", None),
        P("dp"),
        P("dp", None, None, None),
        P(("dp", "feat"), None),
    )
    out_specs = (P(("dp", "feat"), None), P("feat", None))
    return jax.shard_map(shards, mesh=mesh, in_specs=in_specs, out_specs=out_specs, check_vma=False)
```

```python
import functools

import jax
import jax.numpy as jnp
from jax import lax
from jax.experimental import pallas as pl
from jax.experimental.pallas import tpu as pltpu
from jax.sharding import PartitionSpec as P

MESH = pl.DeviceIdType.MESH
TILE = 128


def around(n):
    return sorted(range(1, n), key=lambda k: (-min(k, n - k), -k))


def slots(n):
    return [0] + around(n)[::-1]


def kernel(
    nx, n, maxt, width, tix_h, tcnt_h, src, weight, mask, cot, hid_out, wg_out,
    tix, tcnt, src_v, src_x, mask_v, w_own, cot_x, w_near, w_ab, agg_send, agg_full, z_send, z_recv,
    p1x_send, p1x_recv, pair_send, pair_recv, lone_send, lone_recv, p2x_send, p2x_recv, p2_send, p2_recv,
    p3_send, p3_recv, res, wg_acc,
    ix_sem, src_sem, mask_sem, w_sem, cot_sem, cx_send, cx_recv, wd_send, wd_recv, w1_send, w1_recv, w2_send, w2_recv,
    a_send, a_recv, z_ss, z_rs, p1x_ss, p1x_rs, pair_ss, pair_rs, lone_ss, lone_rs, p2x_ss, p2x_rs, p2_ss, p2_rs,
    p3_ss, p3_rs, p4_ss, p4_rs,
):
    dp = lax.axis_index("dp")
    feat = lax.axis_index("feat")
    y, z = lax.div(dp, n), lax.rem(dp, n)
    x, c = lax.div(feat, 2), lax.rem(feat, 2)
    half = n // 2
    rows = TILE // n
    rel = slots(nx)
    near = min(3, nx)
    far = [(a, b) for a, b in ((near, min(near + 2, nx)), (near + 2, nx)) if a < b]
    place = (y, z)
    f32, bf16 = jnp.float32, jnp.bfloat16

    def at(ab, i):
        return i * n + z if ab == 0 else y * n + i

    def spot(axis):
        return y + axis * (z - y)

    def to(axis, i):
        return i * n + z + axis * (y * n + i - i * n - z)

    def remote(source, target, ssem, rsem, where):
        return pltpu.make_async_remote_copy(
            src_ref=source, dst_ref=target, send_sem=ssem, recv_sem=rsem, device_id=where, device_id_type=MESH
        )

    def arrived(ref, sem):
        remote(ref, ref, sem, sem, (dp, feat)).wait_recv()

    def left(ref, sem):
        remote(ref, ref, sem, sem, (dp, feat)).wait_send()

    def each(count, body):
        def step(i, carry):
            body(i)
            return carry

        lax.fori_loop(0, count, step, 0)

    def served(step):
        off = jnp.where(lax.rem(step, 2) == 1, lax.div(nx - 1 - step, 2), nx // 2 + lax.div(step, 2))
        return off

    def mask_copy(step):
        chip = lax.rem(x + served(step), nx)
        return pltpu.make_async_copy(mask.at[pl.ds(2 * chip, 2)], mask_v.at[step], mask_sem.at[step])

    barrier = pltpu.get_barrier_semaphore()

    def greet(where):
        pl.semaphore_signal(barrier, inc=1, device_id=where, device_id_type=MESH)

    get_w = pltpu.make_async_copy(weight, w_own, w_sem)
    get_ix = [pltpu.make_async_copy(a, b, ix_sem.at[i]) for i, (a, b) in enumerate(((tix_h, tix), (tcnt_h, tcnt)))]
    get_src = pltpu.make_async_copy(src, src_v, src_sem)
    get_cot = pltpu.make_async_copy(cot, cot_x.at[c], cot_sem)
    for copy in (get_w, *get_ix, get_src):
        copy.start()
    for k in range(2):
        mask_copy(jnp.int32(k)).start()
    for off in around(nx):
        greet((dp, 2 * lax.rem(x + off, nx) + c))
    greet((dp, 2 * x + 1 - c))
    for off in around(n):
        for ab in (0, 1):
            greet((at(ab, lax.rem(place[ab] + off, n)), feat))
    for k in range(2, nx):
        mask_copy(jnp.int32(k)).start()
    get_cot.start()

    def chip_at(steps):
        return lax.rem(x + nx + steps, nx)

    def wd_copy(slot):
        return remote(w_own, w_near.at[slot], wd_send, wd_recv, (dp, 2 * chip_at(-rel[slot]) + c))

    def w1_copy(ab, slot):
        column = pl.multiple_of((2 * ab + lax.div(place[ab], half)) * TILE, TILE)
        return remote(
            w_own.at[lax.rem(place[ab], half), :, pl.ds(column, TILE)],
            w_ab.at[ab, slot, place[ab]],
            w1_send.at[ab],
            w1_recv.at[ab, [k for k, (a, b) in enumerate(far) if a <= slot < b][0]],
            (dp, 2 * chip_at(-rel[slot]) + c),
        )

    def w2_copy(ab, group, i):
        piece = w_ab.at[ab, far[group][0] : far[group][1], place[ab]]
        return remote(piece, piece, w2_send.at[ab, group], w2_recv.at[ab, group], (at(ab, i), feat))

    def others(ab, body):
        for off in around(n):
            body(lax.rem(place[ab] + off, n))

    def send_w2(group):
        for ab in (0, 1):
            arrived(w_ab.at[ab, far[group][0] : far[group][1], place[ab]], w1_recv.at[ab, group])
            others(ab, lambda i, ab=ab: w2_copy(ab, group, i).start())

    def cot_copy():
        return remote(cot_x.at[c], cot_x.at[c], cx_send, cx_recv, (dp, 2 * x + 1 - c))

    def a_copy(step, to_x):
        slot = nx - 1 - step
        return remote(agg_send.at[step], agg_full.at[slot], a_send, a_recv, (dp, 2 * to_x + c))

    def aggregate(step, k, chip):
        b = 2 * chip + k
        count = tcnt[0, b]
        links, picks = [], []
        for s in range(maxt):
            links.append(mask_v[step, k, s].astype(f32).astype(bf16))
            picks.append(jnp.where(s < count, src_x[tix[s, b]], jnp.zeros((), bf16)))
        total = lax.dot_general(
            jnp.concatenate(picks, axis=1),
            jnp.concatenate(links, axis=1),
            (((1,), (1,)), ((), ())),
            preferred_element_type=f32,
        )
        return (total[:width] / jnp.maximum(total[width : width + 1], 1.0)).astype(bf16)

    def chip_step(step):
        chip = lax.rem(x + served(step), nx)
        mask_copy(step).wait()
        for k in (0, 1):
            agg_send[step, :, k * TILE : (k + 1) * TILE] = aggregate(step, k, chip)

        @pl.when(step < nx - 1)
        def _():
            a_copy(step, chip).start()

    get_w.wait()
    pl.semaphore_wait(barrier, nx + 2 * (n - 1))
    for slot in reversed(range(near, nx)):
        for ab in (0, 1):
            w1_copy(ab, slot).start()
    for slot in range(1, near):
        wd_copy(slot).start()
    get_cot.wait()
    cot_copy().start()
    for copy in get_ix:
        copy.wait()
    get_src.wait()
    ones = jnp.ones((16, TILE), bf16)
    for i in range(src_x.shape[0]):
        src_x[i] = jnp.concatenate([src_v[:, i * TILE : (i + 1) * TILE], ones], axis=0)
    each(nx, chip_step)
    agg_full[0] = agg_send[nx - 1]

    for group in range(len(far)):
        send_w2(group)

    arrived(cot_x.at[1 - c], cx_recv)
    cot_all = cot_x[...].reshape(2 * TILE, 4 * TILE).astype(f32)
    w_near[0] = w_own[...]
    arrived(w_near.at[1:near], wd_recv)
    arrived(agg_full.at[1:nx], a_recv)
    agg = agg_full[...].reshape(nx * width, 2 * TILE)
    agg_t = agg.T
    pieces = [w_near[slot].reshape(width, 4 * TILE) for slot in range(near)]
    for group, (first, last) in enumerate(far):
        for ab in (0, 1):
            arrived(w_ab.at[ab, first:last, 0 : n - 1], w2_recv.at[ab, group])
        for slot in range(first, last):
            columns = [w_ab[ab, slot, k * half : (k + 1) * half] for ab in (0, 1) for k in (0, 1)]
            pieces.append(jnp.concatenate([piece.reshape(width, TILE) for piece in columns], axis=1))
    part = jnp.dot(agg_t, jnp.concatenate(pieces, axis=0), preferred_element_type=f32)
    z_send[...] = part.astype(bf16)
    z_copy = remote(z_send, z_recv, z_ss, z_rs, (dp, 2 * x + 1 - c))
    z_copy.start()
    z_copy.wait()
    zt = part + z_recv[...].astype(f32)
    sig = jax.nn.sigmoid(zt)
    dz = (cot_all * sig * (1.0 + zt * (1.0 - sig))).astype(bf16)
    hid = zt * sig

    r = TILE // 2 // n

    def pair_copy(i):
        return remote(pair_send.at[i], pair_recv.at[spot(c)], pair_ss, pair_rs, (to(c, i), feat))

    def lone_copy(i):
        return remote(lone_send.at[i], lone_recv.at[spot(1 - c)], lone_ss, lone_rs, (to(1 - c, i), feat))

    def p2x_copy(i):
        return remote(p2x_send.at[i], p2x_recv.at[spot(1 - c)], p2x_ss, p2x_rs, (to(1 - c, i), feat))

    def along(axis, body):
        for off in around(n):
            body(lax.rem(spot(axis) + off, n))

    def slot_copy(send, recv, ssem, rsem, slot):
        return remote(send.at[slot], recv.at[slot], ssem, rsem, (dp, 2 * chip_at(rel[slot]) + c))

    p1x_copy = functools.partial(slot_copy, p1x_send, p1x_recv, p1x_ss, p1x_rs)
    p2_copy = functools.partial(slot_copy, p2_send, p2_recv, p2_ss, p2_rs)

    for group in range(4):
        part = jnp.dot(agg, dz[:, group * TILE : (group + 1) * TILE], preferred_element_type=f32)
        if group == 0:
            p1x_send[...] = part.reshape(nx, width, TILE).astype(bf16)
            continue
        part = part.reshape(nx, n, r, TILE)
        for i in range(n):
            piece = part[:, i].reshape(nx // 2, 2 * r, TILE).astype(bf16)
            if group == 1:
                lone_send[i] = piece
            else:
                pair_send[i, group - 2] = piece
    for step in range(max(n, nx) - 1):
        if step < n - 1:
            pair_copy(lax.rem(spot(c) + around(n)[step], n)).start()
            lone_copy(lax.rem(spot(1 - c) + around(n)[step], n)).start()
        if step < nx - 1:
            p1x_copy(nx - 1 - step).start()

    hid_out[...] = jnp.where(c == 0, hid[:TILE], hid[TILE:]).astype(bf16)
    if far:
        for ab in (0, 1):
            left(w_ab.at[ab, near:nx, 0], w1_send.at[ab])
    for group, (first, last) in enumerate(far):
        for ab in (0, 1):
            left(w_ab.at[ab, first:last, 0 : n - 1], w2_send.at[ab, group])
    left(w_near.at[1:near], wd_send)
    left(cot_x.at[0], cx_send)
    left(agg_send.at[0 : nx - 1], a_send)

    p1x_recv[0] = p1x_send[0]
    arrived(p1x_recv.at[1:nx], p1x_rs)
    p2x_send[...] = jnp.sum(p1x_recv[...].astype(f32), axis=0).reshape(n, r, TILE)
    along(1 - c, lambda i: p2x_copy(i).start())
    lone_recv[spot(1 - c)] = lone_send[spot(1 - c)]
    arrived(lone_recv.at[0 : n - 1], lone_rs)
    p2_send[:, 2] = jnp.sum(lone_recv[...].astype(f32), axis=0).reshape(nx, r, TILE)
    pair_recv[spot(c)] = pair_send[spot(c)]
    arrived(pair_recv.at[0 : n - 1], pair_rs)
    for k in (0, 1):
        p2_send[:, k] = jnp.sum(pair_recv[:, k].astype(f32), axis=0).reshape(nx, r, TILE)
    for slot in reversed(range(1, nx)):
        p2_copy(slot).start()
    left(p1x_send.at[1:nx], p1x_ss)
    left(pair_send.at[0 : n - 1], pair_ss)
    left(lone_send.at[0 : n - 1], lone_ss)
    p2x_recv[spot(1 - c)] = p2x_send[spot(1 - c)]
    arrived(p2x_recv.at[0 : n - 1], p2x_rs)
    group0 = jnp.sum(p2x_recv[...], axis=0)
    p2_recv[0] = p2_send[0]
    arrived(p2_recv.at[1:nx], p2_rs)
    groups = jnp.sum(p2_recv[...], axis=0)

    cuts = (1 - c, c)
    pairs = ((group0, groups[2]), (groups[0], groups[1]))
    for q in (0, 1):
        p3_send[q] = jnp.concatenate(pairs[q], axis=0).astype(bf16)

    def p3_copy(q, i):
        axis = 1 - cuts[q]
        return remote(p3_send.at[q], p3_recv.at[q, spot(axis)], p3_ss.at[q], p3_rs.at[q], (to(axis, i), feat))

    for off in around(n):
        for q in (0, 1):
            p3_copy(q, lax.rem(spot(1 - cuts[q]) + off, n)).start()
    left(p2x_send.at[0 : n - 1], p2x_ss)
    left(p2_send.at[1:nx], p2_ss)
    for q in (0, 1):
        p3_recv[q, spot(1 - cuts[q])] = p3_send[q]
        arrived(p3_recv.at[q, 0 : n - 1], p3_rs.at[q])
        res[q] = jnp.sum(p3_recv[q].astype(f32), axis=0).reshape(2, r, TILE)

    def p4_copy(q, i):
        return remote(res.at[q], wg_acc.at[spot(cuts[q]), q], p4_ss.at[q], p4_rs.at[q], (to(cuts[q], i), feat))

    for off in around(n):
        for q in (0, 1):
            p4_copy(q, lax.rem(spot(cuts[q]) + off, n)).start()
    for q in (0, 1):
        wg_acc[spot(cuts[q]), q] = res[q]
    for q in (0, 1):
        left(p3_recv.at[q, 0 : n - 1], p3_ss.at[q])
    for q in (0, 1):
        left(wg_acc.at[0 : n - 1, q], p4_ss.at[q])
    for q in (0, 1):
        arrived(wg_acc.at[0 : n - 1, q], p4_rs.at[q])
        for i in range(n):
            for k in (0, 1):
                block = 2 * q + k
                wg_out[i * r : (i + 1) * r, block * TILE : (block + 1) * TILE] = wg_acc[i, q, k]


def solution(mesh):
    nx = mesh.shape["feat"] // 2
    n = round(mesh.shape["dp"] ** 0.5)

    def shards(source_feat, weight, tile_index, tile_count, tile_mask, cotangent):
        nblk, maxt, tile, _ = tile_mask.shape
        width = source_feat.shape[1]
        hid = weight.shape[1]
        rows = TILE // n
        half = n // 2
        bf16, f32 = jnp.bfloat16, jnp.float32
        dma = lambda *shape: pltpu.SemaphoreType.DMA(shape)
        vm = pltpu.VMEM
        hbm = pl.BlockSpec(memory_space=pltpu.HBM)
        vmem = pl.BlockSpec(memory_space=pltpu.VMEM)
        hidden, weight_grad = pl.pallas_call(
            functools.partial(kernel, nx, n, maxt, width),
            out_shape=(
                vm((tile, hid), bf16),
                vm((width, hid), f32),
            ),
            in_specs=[hbm] * 6,
            out_specs=(vmem, vmem),
            scratch_shapes=[
                pltpu.SMEM((maxt, nblk), jnp.int32),
                pltpu.SMEM((1, nblk), jnp.int32),
                vm((width, source_feat.shape[0]), bf16),
                vm((source_feat.shape[0] // tile, width + 16, tile), bf16),
                vm((nx, 2, maxt, tile, tile), jnp.int32),
                vm((half, rows, hid), bf16),
                vm((2, tile, hid), bf16),
                vm((min(3, nx), half, rows, hid), bf16),
                vm((2, nx, n, rows, TILE), bf16),
                vm((nx, width, 2 * tile), bf16),
                vm((nx, width, 2 * tile), bf16),
                vm((2 * tile, hid), bf16),
                vm((2 * tile, hid), bf16),
                vm((nx, TILE // 2, TILE), bf16),
                vm((nx, TILE // 2, TILE), bf16),
                vm((n, 2, nx // 2, rows, TILE), bf16),
                vm((n, 2, nx // 2, rows, TILE), bf16),
                vm((n, nx // 2, rows, TILE), bf16),
                vm((n, nx // 2, rows, TILE), bf16),
                vm((n, rows // 2, TILE), f32),
                vm((n, rows // 2, TILE), f32),
                vm((nx, 3, rows // 2, TILE), f32),
                vm((nx, 3, rows // 2, TILE), f32),
                vm((2, rows, TILE), bf16),
                vm((2, n, rows, TILE), bf16),
                vm((2, 2, rows // 2, TILE), f32),
                vm((n, 2, 2, rows // 2, TILE), f32),
                dma(2), dma(), dma(nx), dma(), dma(),
                dma(), dma(),
                dma(), dma(),
                dma(2), dma(2, 2),
                dma(2, 2), dma(2, 2),
                dma(), dma(),
                dma(), dma(),
                dma(), dma(),
                dma(), dma(),
                dma(), dma(),
                dma(), dma(),
                dma(), dma(),
                dma(2), dma(2),
                dma(2), dma(2),
            ],
            compiler_params=pltpu.CompilerParams(
                collective_id=0, has_side_effects=True, vmem_limit_bytes=40 * 1024 * 1024
            ),
        )(
            *(
                pltpu.with_memory_space_constraint(a, pltpu.HBM)
                for a in (
                    tile_index.T,
                    tile_count.reshape(1, nblk),
                    source_feat.T,
                    weight.reshape(half, rows, hid),
                    tile_mask,
                    cotangent,
                )
            )
        )
        return hidden, weight_grad

    in_specs = (
        P("dp", "feat"),
        P("feat", None),
        P("dp", None),
        P("dp"),
        P("dp", None, None, None),
        P(("dp", "feat"), None),
    )
    out_specs = (P(("dp", "feat"), None), P("feat", None))
    return jax.shard_map(shards, mesh=mesh, in_specs=in_specs, out_specs=out_specs, check_vma=False)
```

```python
import functools

import jax
import jax.numpy as jnp
from jax import lax
from jax.experimental import pallas as pl
from jax.experimental.pallas import tpu as pltpu
from jax.sharding import PartitionSpec as P

MESH = pl.DeviceIdType.MESH
TILE = 128


def around(n):
    return sorted(range(1, n), key=lambda k: (-min(k, n - k), -k))


def slots(n):
    return [0] + around(n)[::-1]


def kernel(
    nx, n, maxt, width, tix_h, tcnt_h, src, weight, mask, cot, hid_out, wg_out,
    tix, tcnt, src_v, src_x, mask_v, w_own, cot_x, w_near, w_ab, agg_send, agg_full, z_send, z_recv,
    p1x_send, p1x_recv, pair_send, pair_recv, lone_send, lone_recv, p2x_send, p2x_recv, p2_send, p2_recv,
    p3_send, p3_recv, res, wg_acc,
    ix_sem, src_sem, mask_sem, w_sem, cot_sem, cx_send, cx_recv, wd_send, wd_recv, w1_send, w1_recv, w2_send, w2_recv,
    a_send, a_recv, z_ss, z_rs, p1x_ss, p1x_rs, pair_ss, pair_rs, lone_ss, lone_rs, p2x_ss, p2x_rs, p2_ss, p2_rs,
    p3_ss, p3_rs, p4_ss, p4_rs,
):
    dp = lax.axis_index("dp")
    feat = lax.axis_index("feat")
    y, z = lax.div(dp, n), lax.rem(dp, n)
    x, c = lax.div(feat, 2), lax.rem(feat, 2)
    half = n // 2
    rows = TILE // n
    rel = slots(nx)
    near = min(3, nx)
    far = [(a, b) for a, b in ((near, min(near + 2, nx)), (near + 2, nx)) if a < b]
    place = (y, z)
    f32, bf16 = jnp.float32, jnp.bfloat16

    def at(ab, i):
        return i * n + z if ab == 0 else y * n + i

    def spot(axis):
        return y + axis * (z - y)

    def to(axis, i):
        return i * n + z + axis * (y * n + i - i * n - z)

    def remote(source, target, ssem, rsem, where):
        return pltpu.make_async_remote_copy(
            src_ref=source, dst_ref=target, send_sem=ssem, recv_sem=rsem, device_id=where, device_id_type=MESH
        )

    def arrived(ref, sem):
        remote(ref, ref, sem, sem, (dp, feat)).wait_recv()

    def left(ref, sem):
        remote(ref, ref, sem, sem, (dp, feat)).wait_send()

    def each(count, body):
        def step(i, carry):
            body(i)
            return carry

        lax.fori_loop(0, count, step, 0)

    def served(step):
        off = jnp.where(lax.rem(step, 2) == 1, lax.div(nx - 1 - step, 2), nx // 2 + lax.div(step, 2))
        return off

    def mask_copy(step):
        chip = lax.rem(x + served(step), nx)
        return pltpu.make_async_copy(mask.at[pl.ds(2 * chip, 2)], mask_v.at[step], mask_sem.at[step])

    barrier = pltpu.get_barrier_semaphore()

    def greet(where):
        pl.semaphore_signal(barrier, inc=1, device_id=where, device_id_type=MESH)

    get_w = pltpu.make_async_copy(weight, w_own, w_sem)
    get_ix = [pltpu.make_async_copy(a, b, ix_sem.at[i]) for i, (a, b) in enumerate(((tix_h, tix), (tcnt_h, tcnt)))]
    get_src = pltpu.make_async_copy(src, src_v, src_sem)
    get_cot = pltpu.make_async_copy(cot, cot_x.at[c], cot_sem)
    for copy in (get_w, *get_ix, get_src, get_cot):
        copy.start()
    for k in range(2):
        mask_copy(jnp.int32(k)).start()
    for off in around(nx):
        greet((dp, 2 * lax.rem(x + off, nx) + c))
    greet((dp, 2 * x + 1 - c))
    for off in around(n):
        for ab in (0, 1):
            greet((at(ab, lax.rem(place[ab] + off, n)), feat))
    for k in range(2, nx):
        mask_copy(jnp.int32(k)).start()

    def chip_at(steps):
        return lax.rem(x + nx + steps, nx)

    def wd_copy(slot):
        return remote(w_own, w_near.at[slot], wd_send, wd_recv, (dp, 2 * chip_at(-rel[slot]) + c))

    def w1_copy(ab, slot):
        column = pl.multiple_of((2 * ab + lax.div(place[ab], half)) * TILE, TILE)
        return remote(
            w_own.at[lax.rem(place[ab], half), :, pl.ds(column, TILE)],
            w_ab.at[ab, slot, place[ab]],
            w1_send.at[ab],
            w1_recv.at[ab, [k for k, (a, b) in enumerate(far) if a <= slot < b][0]],
            (dp, 2 * chip_at(-rel[slot]) + c),
        )

    def w2_copy(ab, group, i):
        piece = w_ab.at[ab, far[group][0] : far[group][1], place[ab]]
        return remote(piece, piece, w2_send.at[ab, group], w2_recv.at[ab, group], (at(ab, i), feat))

    def others(ab, body):
        for off in around(n):
            body(lax.rem(place[ab] + off, n))

    def send_w2(group):
        for ab in (0, 1):
            arrived(w_ab.at[ab, far[group][0] : far[group][1], place[ab]], w1_recv.at[ab, group])
            others(ab, lambda i, ab=ab: w2_copy(ab, group, i).start())

    def cot_copy():
        return remote(cot_x.at[c], cot_x.at[c], cx_send, cx_recv, (dp, 2 * x + 1 - c))

    def a_copy(step, to_x):
        slot = nx - 1 - step
        return remote(agg_send.at[step], agg_full.at[slot], a_send, a_recv, (dp, 2 * to_x + c))

    def aggregate(step, k, chip):
        b = 2 * chip + k
        count = tcnt[0, b]
        links, picks = [], []
        for s in range(maxt):
            links.append(mask_v[step, k, s].astype(f32).astype(bf16))
            picks.append(jnp.where(s < count, src_x[tix[s, b]], jnp.zeros((), bf16)))
        total = lax.dot_general(
            jnp.concatenate(picks, axis=1),
            jnp.concatenate(links, axis=1),
            (((1,), (1,)), ((), ())),
            preferred_element_type=f32,
        )
        return (total[:width] / jnp.maximum(total[width : width + 1], 1.0)).astype(bf16)

    def chip_step(step):
        chip = lax.rem(x + served(step), nx)
        mask_copy(step).wait()
        for k in (0, 1):
            agg_send[step, :, k * TILE : (k + 1) * TILE] = aggregate(step, k, chip)

        @pl.when(step < nx - 1)
        def _():
            a_copy(step, chip).start()

    get_w.wait()
    pl.semaphore_wait(barrier, nx + 2 * (n - 1))
    for slot in reversed(range(near, nx)):
        for ab in (0, 1):
            w1_copy(ab, slot).start()
    for slot in range(1, near):
        wd_copy(slot).start()
    get_cot.wait()
    cot_copy().start()
    for copy in get_ix:
        copy.wait()
    get_src.wait()
    ones = jnp.ones((16, TILE), bf16)
    for i in range(src_x.shape[0]):
        src_x[i] = jnp.concatenate([src_v[:, i * TILE : (i + 1) * TILE], ones], axis=0)
    each(nx, chip_step)
    agg_full[0] = agg_send[nx - 1]

    for group in range(len(far)):
        send_w2(group)

    arrived(cot_x.at[1 - c], cx_recv)
    cot_all = cot_x[...].reshape(2 * TILE, 4 * TILE).astype(f32)
    w_near[0] = w_own[...]
    arrived(w_near.at[1:near], wd_recv)
    arrived(agg_full.at[1:nx], a_recv)
    agg = agg_full[...].reshape(nx * width, 2 * TILE)
    agg_t = agg.T
    pieces = [w_near[slot].reshape(width, 4 * TILE) for slot in range(near)]
    for group, (first, last) in enumerate(far):
        for ab in (0, 1):
            arrived(w_ab.at[ab, first:last, 0 : n - 1], w2_recv.at[ab, group])
        for slot in range(first, last):
            columns = [w_ab[ab, slot, k * half : (k + 1) * half] for ab in (0, 1) for k in (0, 1)]
            pieces.append(jnp.concatenate([piece.reshape(width, TILE) for piece in columns], axis=1))
    part = jnp.dot(agg_t, jnp.concatenate(pieces, axis=0), preferred_element_type=f32)
    z_send[...] = part.astype(bf16)
    z_copy = remote(z_send, z_recv, z_ss, z_rs, (dp, 2 * x + 1 - c))
    z_copy.start()
    z_copy.wait()
    zt = part + z_recv[...].astype(f32)
    sig = jax.nn.sigmoid(zt)
    dz = (cot_all * sig * (1.0 + zt * (1.0 - sig))).astype(bf16)
    hid = zt * sig

    r = TILE // 2 // n

    def pair_copy(i):
        return remote(pair_send.at[i], pair_recv.at[spot(c)], pair_ss, pair_rs, (to(c, i), feat))

    def lone_copy(i):
        return remote(lone_send.at[i], lone_recv.at[spot(1 - c)], lone_ss, lone_rs, (to(1 - c, i), feat))

    def p2x_copy(i):
        return remote(p2x_send.at[i], p2x_recv.at[spot(1 - c)], p2x_ss, p2x_rs, (to(1 - c, i), feat))

    def along(axis, body):
        for off in around(n):
            body(lax.rem(spot(axis) + off, n))

    def slot_copy(send, recv, ssem, rsem, slot):
        return remote(send.at[slot], recv.at[slot], ssem, rsem, (dp, 2 * chip_at(rel[slot]) + c))

    p1x_copy = functools.partial(slot_copy, p1x_send, p1x_recv, p1x_ss, p1x_rs)
    p2_copy = functools.partial(slot_copy, p2_send, p2_recv, p2_ss, p2_rs)

    for group in range(4):
        part = jnp.dot(agg, dz[:, group * TILE : (group + 1) * TILE], preferred_element_type=f32)
        if group == 0:
            p1x_send[...] = part.reshape(nx, width, TILE).astype(bf16)
            continue
        part = part.reshape(nx, n, r, TILE)
        for i in range(n):
            piece = part[:, i].reshape(nx // 2, 2 * r, TILE).astype(bf16)
            if group == 1:
                lone_send[i] = piece
            else:
                pair_send[i, group - 2] = piece
    for step in range(max(n, nx) - 1):
        if step < n - 1:
            pair_copy(lax.rem(spot(c) + around(n)[step], n)).start()
            lone_copy(lax.rem(spot(1 - c) + around(n)[step], n)).start()
        if step < nx - 1:
            p1x_copy(nx - 1 - step).start()

    hid_out[...] = jnp.where(c == 0, hid[:TILE], hid[TILE:]).astype(bf16)
    if far:
        for ab in (0, 1):
            left(w_ab.at[ab, near:nx, 0], w1_send.at[ab])
    for group, (first, last) in enumerate(far):
        for ab in (0, 1):
            left(w_ab.at[ab, first:last, 0 : n - 1], w2_send.at[ab, group])
    left(w_near.at[1:near], wd_send)
    left(cot_x.at[0], cx_send)
    left(agg_send.at[0 : nx - 1], a_send)

    p1x_recv[0] = p1x_send[0]
    arrived(p1x_recv.at[1:nx], p1x_rs)
    p2x_send[...] = jnp.sum(p1x_recv[...].astype(f32), axis=0).reshape(n, r, TILE)
    along(1 - c, lambda i: p2x_copy(i).start())
    lone_recv[spot(1 - c)] = lone_send[spot(1 - c)]
    arrived(lone_recv.at[0 : n - 1], lone_rs)
    p2_send[:, 2] = jnp.sum(lone_recv[...].astype(f32), axis=0).reshape(nx, r, TILE)
    pair_recv[spot(c)] = pair_send[spot(c)]
    arrived(pair_recv.at[0 : n - 1], pair_rs)
    for k in (0, 1):
        p2_send[:, k] = jnp.sum(pair_recv[:, k].astype(f32), axis=0).reshape(nx, r, TILE)
    for slot in reversed(range(1, nx)):
        p2_copy(slot).start()
    left(p1x_send.at[1:nx], p1x_ss)
    left(pair_send.at[0 : n - 1], pair_ss)
    left(lone_send.at[0 : n - 1], lone_ss)
    p2x_recv[spot(1 - c)] = p2x_send[spot(1 - c)]
    arrived(p2x_recv.at[0 : n - 1], p2x_rs)
    group0 = jnp.sum(p2x_recv[...], axis=0)
    p2_recv[0] = p2_send[0]
    arrived(p2_recv.at[1:nx], p2_rs)
    groups = jnp.sum(p2_recv[...], axis=0)

    cuts = (1 - c, c)
    pairs = ((group0, groups[2]), (groups[0], groups[1]))
    for q in (0, 1):
        p3_send[q] = jnp.concatenate(pairs[q], axis=0).astype(bf16)

    def p3_copy(q, i):
        axis = 1 - cuts[q]
        return remote(p3_send.at[q], p3_recv.at[q, spot(axis)], p3_ss.at[q], p3_rs.at[q], (to(axis, i), feat))

    for off in around(n):
        for q in (0, 1):
            p3_copy(q, lax.rem(spot(1 - cuts[q]) + off, n)).start()
    left(p2x_send.at[0 : n - 1], p2x_ss)
    left(p2_send.at[1:nx], p2_ss)
    for q in (0, 1):
        p3_recv[q, spot(1 - cuts[q])] = p3_send[q]
        arrived(p3_recv.at[q, 0 : n - 1], p3_rs.at[q])
        res[q] = jnp.sum(p3_recv[q].astype(f32), axis=0).reshape(2, r, TILE)

    def p4_copy(q, i):
        return remote(res.at[q], wg_acc.at[spot(cuts[q]), q], p4_ss.at[q], p4_rs.at[q], (to(cuts[q], i), feat))

    for off in around(n):
        for q in (0, 1):
            p4_copy(q, lax.rem(spot(cuts[q]) + off, n)).start()
    for q in (0, 1):
        wg_acc[spot(cuts[q]), q] = res[q]
    for q in (0, 1):
        left(p3_recv.at[q, 0 : n - 1], p3_ss.at[q])
    for q in (0, 1):
        left(wg_acc.at[0 : n - 1, q], p4_ss.at[q])
    for q in (0, 1):
        arrived(wg_acc.at[0 : n - 1, q], p4_rs.at[q])
        for i in range(n):
            for k in (0, 1):
                block = 2 * q + k
                wg_out[i * r : (i + 1) * r, block * TILE : (block + 1) * TILE] = wg_acc[i, q, k]


def solution(mesh):
    nx = mesh.shape["feat"] // 2
    n = round(mesh.shape["dp"] ** 0.5)

    def shards(source_feat, weight, tile_index, tile_count, tile_mask, cotangent):
        nblk, maxt, tile, _ = tile_mask.shape
        width = source_feat.shape[1]
        hid = weight.shape[1]
        rows = TILE // n
        half = n // 2
        bf16, f32 = jnp.bfloat16, jnp.float32
        dma = lambda *shape: pltpu.SemaphoreType.DMA(shape)
        vm = pltpu.VMEM
        hbm = pl.BlockSpec(memory_space=pltpu.HBM)
        vmem = pl.BlockSpec(memory_space=pltpu.VMEM)
        hidden, weight_grad = pl.pallas_call(
            functools.partial(kernel, nx, n, maxt, width),
            out_shape=(
                vm((tile, hid), bf16),
                vm((width, hid), f32),
            ),
            in_specs=[hbm] * 6,
            out_specs=(vmem, vmem),
            scratch_shapes=[
                pltpu.SMEM((maxt, nblk), jnp.int32),
                pltpu.SMEM((1, nblk), jnp.int32),
                vm((width, source_feat.shape[0]), bf16),
                vm((source_feat.shape[0] // tile, width + 16, tile), bf16),
                vm((nx, 2, maxt, tile, tile), jnp.int32),
                vm((half, rows, hid), bf16),
                vm((2, tile, hid), bf16),
                vm((min(3, nx), half, rows, hid), bf16),
                vm((2, nx, n, rows, TILE), bf16),
                vm((nx, width, 2 * tile), bf16),
                vm((nx, width, 2 * tile), bf16),
                vm((2 * tile, hid), bf16),
                vm((2 * tile, hid), bf16),
                vm((nx, TILE // 2, TILE), bf16),
                vm((nx, TILE // 2, TILE), bf16),
                vm((n, 2, nx // 2, rows, TILE), bf16),
                vm((n, 2, nx // 2, rows, TILE), bf16),
                vm((n, nx // 2, rows, TILE), bf16),
                vm((n, nx // 2, rows, TILE), bf16),
                vm((n, rows // 2, TILE), f32),
                vm((n, rows // 2, TILE), f32),
                vm((nx, 3, rows // 2, TILE), f32),
                vm((nx, 3, rows // 2, TILE), f32),
                vm((2, rows, TILE), bf16),
                vm((2, n, rows, TILE), bf16),
                vm((2, 2, rows // 2, TILE), f32),
                vm((n, 2, 2, rows // 2, TILE), f32),
                dma(2), dma(), dma(nx), dma(), dma(),
                dma(), dma(),
                dma(), dma(),
                dma(2), dma(2, 2),
                dma(2, 2), dma(2, 2),
                dma(), dma(),
                dma(), dma(),
                dma(), dma(),
                dma(), dma(),
                dma(), dma(),
                dma(), dma(),
                dma(), dma(),
                dma(2), dma(2),
                dma(2), dma(2),
            ],
            compiler_params=pltpu.CompilerParams(
                collective_id=0, has_side_effects=True, vmem_limit_bytes=40 * 1024 * 1024
            ),
        )(
            *(
                pltpu.with_memory_space_constraint(a, pltpu.HBM)
                for a in (
                    tile_index.T,
                    tile_count.reshape(1, nblk),
                    source_feat.T,
                    weight.reshape(half, rows, hid),
                    tile_mask,
                    cotangent,
                )
            )
        )
        return hidden, weight_grad

    in_specs = (
        P("dp", "feat"),
        P("feat", None),
        P("dp", None),
        P("dp"),
        P("dp", None, None, None),
        P(("dp", "feat"), None),
    )
    out_specs = (P(("dp", "feat"), None), P("feat", None))
    return jax.shard_map(shards, mesh=mesh, in_specs=in_specs, out_specs=out_specs, check_vma=False)
```

```python
import functools

import jax
import jax.numpy as jnp
from jax import lax
from jax.experimental import pallas as pl
from jax.experimental.pallas import tpu as pltpu
from jax.sharding import PartitionSpec as P

MESH = pl.DeviceIdType.MESH
TILE = 128


def around(n):
    return sorted(range(1, n), key=lambda k: (-min(k, n - k), -k))


def slots(n):
    return [0] + around(n)[::-1]


def kernel(
    nx, n, maxt, width, tix_h, tcnt_h, src, weight, mask, cot, hid_out, wg_out,
    tix, tcnt, src_v, src_x, mask_v, w_own, cot_x, w_near, w_ab, agg_send, agg_full, z_send, z_recv,
    p1x_send, p1x_recv, pair_send, pair_recv, lone_send, lone_recv, p2x_send, p2x_recv, p2_send, p2_recv,
    p3_send, p3_recv, res, wg_acc,
    ix_sem, src_sem, mask_sem, w_sem, cot_sem, cx_send, cx_recv, wd_send, wd_recv, w1_send, w1_recv, w2_send, w2_recv,
    a_send, a_recv, z_ss, z_rs, p1x_ss, p1x_rs, pair_ss, pair_rs, lone_ss, lone_rs, p2x_ss, p2x_rs, p2_ss, p2_rs,
    p3_ss, p3_rs, p4_ss, p4_rs,
):
    dp = lax.axis_index("dp")
    feat = lax.axis_index("feat")
    y, z = lax.div(dp, n), lax.rem(dp, n)
    x, c = lax.div(feat, 2), lax.rem(feat, 2)
    half = n // 2
    rows = TILE // n
    rel = slots(nx)
    near = min(3, nx)
    far = [(a, b) for a, b in ((near, min(near + 2, nx)), (near + 2, nx)) if a < b]
    place = (y, z)
    f32, bf16 = jnp.float32, jnp.bfloat16

    def at(ab, i):
        return i * n + z if ab == 0 else y * n + i

    def spot(axis):
        return y + axis * (z - y)

    def to(axis, i):
        return i * n + z + axis * (y * n + i - i * n - z)

    def remote(source, target, ssem, rsem, where):
        return pltpu.make_async_remote_copy(
            src_ref=source, dst_ref=target, send_sem=ssem, recv_sem=rsem, device_id=where, device_id_type=MESH
        )

    def arrived(ref, sem):
        remote(ref, ref, sem, sem, (dp, feat)).wait_recv()

    def left(ref, sem):
        remote(ref, ref, sem, sem, (dp, feat)).wait_send()

    def each(count, body):
        def step(i, carry):
            body(i)
            return carry

        lax.fori_loop(0, count, step, 0)

    def served(step):
        off = jnp.where(lax.rem(step, 2) == 1, lax.div(nx - 1 - step, 2), nx // 2 + lax.div(step, 2))
        return off

    def mask_copy(step):
        chip = lax.rem(x + served(step), nx)
        return pltpu.make_async_copy(mask.at[pl.ds(2 * chip, 2)], mask_v.at[step], mask_sem.at[step])

    barrier = pltpu.get_barrier_semaphore()

    def greet(where):
        pl.semaphore_signal(barrier, inc=1, device_id=where, device_id_type=MESH)

    get_w = pltpu.make_async_copy(weight, w_own, w_sem)
    get_ix = [pltpu.make_async_copy(a, b, ix_sem.at[i]) for i, (a, b) in enumerate(((tix_h, tix), (tcnt_h, tcnt)))]
    get_src = pltpu.make_async_copy(src, src_v, src_sem)
    get_cot = pltpu.make_async_copy(cot, cot_x.at[c], cot_sem)
    for copy in (get_w, *get_ix, get_src, get_cot):
        copy.start()
    for k in range(2):
        mask_copy(jnp.int32(k)).start()
    for off in around(nx):
        greet((dp, 2 * lax.rem(x + off, nx) + c))
    greet((dp, 2 * x + 1 - c))
    for off in around(n):
        for ab in (0, 1):
            greet((at(ab, lax.rem(place[ab] + off, n)), feat))
    for k in range(2, nx):
        mask_copy(jnp.int32(k)).start()

    def chip_at(steps):
        return lax.rem(x + nx + steps, nx)

    def wd_copy(slot):
        return remote(w_own, w_near.at[slot], wd_send, wd_recv, (dp, 2 * chip_at(-rel[slot]) + c))

    def w1_copy(ab, slot):
        column = pl.multiple_of((2 * ab + lax.div(place[ab], half)) * TILE, TILE)
        return remote(
            w_own.at[lax.rem(place[ab], half), :, pl.ds(column, TILE)],
            w_ab.at[ab, slot, place[ab]],
            w1_send.at[ab],
            w1_recv.at[ab, [k for k, (a, b) in enumerate(far) if a <= slot < b][0]],
            (dp, 2 * chip_at(-rel[slot]) + c),
        )

    def w2_copy(ab, group, i):
        piece = w_ab.at[ab, far[group][0] : far[group][1], place[ab]]
        return remote(piece, piece, w2_send.at[ab, group], w2_recv.at[ab, group], (at(ab, i), feat))

    def others(ab, body):
        for off in around(n):
            body(lax.rem(place[ab] + off, n))

    def send_w2(group):
        for ab in (0, 1):
            arrived(w_ab.at[ab, far[group][0] : far[group][1], place[ab]], w1_recv.at[ab, group])
            others(ab, lambda i, ab=ab: w2_copy(ab, group, i).start())

    def cot_copy():
        return remote(cot_x.at[c], cot_x.at[c], cx_send, cx_recv, (dp, 2 * x + 1 - c))

    def a_copy(step, to_x):
        slot = nx - 1 - step
        return remote(agg_send.at[step], agg_full.at[slot], a_send, a_recv, (dp, 2 * to_x + c))

    def aggregate(step, k, chip):
        b = 2 * chip + k
        count = tcnt[0, b]
        links, picks = [], []
        for s in range(maxt):
            links.append(mask_v[step, k, s].astype(f32).astype(bf16))
            picks.append(jnp.where(s < count, src_x[tix[s, b]], jnp.zeros((), bf16)))
        total = lax.dot_general(
            jnp.concatenate(picks, axis=1),
            jnp.concatenate(links, axis=1),
            (((1,), (1,)), ((), ())),
            preferred_element_type=f32,
        )
        return (total[:width] / jnp.maximum(total[width : width + 1], 1.0)).astype(bf16)

    def chip_step(step):
        chip = lax.rem(x + served(step), nx)
        mask_copy(step).wait()
        for k in (0, 1):
            agg_send[step, :, k * TILE : (k + 1) * TILE] = aggregate(step, k, chip)

        @pl.when(step < nx - 1)
        def _():
            a_copy(step, chip).start()

    get_w.wait()
    pl.semaphore_wait(barrier, nx + 2 * (n - 1))
    for slot in reversed(range(near, nx)):
        for ab in (0, 1):
            w1_copy(ab, slot).start()
    for slot in range(1, near):
        wd_copy(slot).start()
    get_cot.wait()
    cot_copy().start()
    for copy in get_ix:
        copy.wait()
    get_src.wait()
    ones = jnp.ones((16, TILE), bf16)
    for i in range(src_x.shape[0]):
        src_x[i] = jnp.concatenate([src_v[:, i * TILE : (i + 1) * TILE], ones], axis=0)
    each(nx, chip_step)
    agg_full[0] = agg_send[nx - 1]

    for group in range(len(far)):
        send_w2(group)

    arrived(cot_x.at[1 - c], cx_recv)
    cot_all = cot_x[...].reshape(2 * TILE, 4 * TILE).astype(f32)
    w_near[0] = w_own[...]
    arrived(w_near.at[1:near], wd_recv)
    arrived(agg_full.at[1:nx], a_recv)
    agg = agg_full[...].reshape(nx * width, 2 * TILE)
    agg_t = agg.T
    pieces = [w_near[slot].reshape(width, 4 * TILE) for slot in range(near)]
    for group, (first, last) in enumerate(far):
        for ab in (0, 1):
            arrived(w_ab.at[ab, first:last, 0 : n - 1], w2_recv.at[ab, group])
        for slot in range(first, last):
            columns = [w_ab[ab, slot, k * half : (k + 1) * half] for ab in (0, 1) for k in (0, 1)]
            pieces.append(jnp.concatenate([piece.reshape(width, TILE) for piece in columns], axis=1))
    part = jnp.dot(agg_t, jnp.concatenate(pieces, axis=0), preferred_element_type=f32)
    z_send[...] = part.astype(bf16)
    z_copy = remote(z_send, z_recv, z_ss, z_rs, (dp, 2 * x + 1 - c))
    z_copy.start()
    z_copy.wait()
    zt = part + z_recv[...].astype(f32)
    sig = jax.nn.sigmoid(zt)
    dz = (cot_all * sig * (1.0 + zt * (1.0 - sig))).astype(bf16)
    hid = zt * sig

    r = TILE // 2 // n

    def pair_copy(i):
        return remote(pair_send.at[i], pair_recv.at[spot(c)], pair_ss, pair_rs, (to(c, i), feat))

    def lone_copy(i):
        return remote(lone_send.at[i], lone_recv.at[spot(1 - c)], lone_ss, lone_rs, (to(1 - c, i), feat))

    def p2x_copy(i):
        return remote(p2x_send.at[i], p2x_recv.at[spot(1 - c)], p2x_ss, p2x_rs, (to(1 - c, i), feat))

    def along(axis, body):
        for off in around(n):
            body(lax.rem(spot(axis) + off, n))

    def slot_copy(send, recv, ssem, rsem, slot):
        return remote(send.at[slot], recv.at[slot], ssem, rsem, (dp, 2 * chip_at(rel[slot]) + c))

    p1x_copy = functools.partial(slot_copy, p1x_send, p1x_recv, p1x_ss, p1x_rs)
    p2_copy = functools.partial(slot_copy, p2_send, p2_recv, p2_ss, p2_rs)

    for group in range(4):
        part = jnp.dot(agg, dz[:, group * TILE : (group + 1) * TILE], preferred_element_type=f32)
        if group == 0:
            p1x_send[...] = part.reshape(nx, width, TILE).astype(bf16)
            continue
        part = part.reshape(nx, n, r, TILE)
        for i in range(n):
            piece = part[:, i].reshape(nx // 2, 2 * r, TILE).astype(bf16)
            if group == 1:
                lone_send[i] = piece
            else:
                pair_send[i, group - 2] = piece
    for step in range(max(n, nx) - 1):
        if step < n - 1:
            pair_copy(lax.rem(spot(c) + around(n)[step], n)).start()
            lone_copy(lax.rem(spot(1 - c) + around(n)[step], n)).start()
        if step < nx - 1:
            p1x_copy(nx - 1 - step).start()

    hid_out[...] = jnp.where(c == 0, hid[:TILE], hid[TILE:]).astype(bf16)
    if far:
        for ab in (0, 1):
            left(w_ab.at[ab, near:nx, 0], w1_send.at[ab])
    for group, (first, last) in enumerate(far):
        for ab in (0, 1):
            left(w_ab.at[ab, first:last, 0 : n - 1], w2_send.at[ab, group])
    left(w_near.at[1:near], wd_send)
    left(cot_x.at[0], cx_send)
    left(agg_send.at[0 : nx - 1], a_send)

    p1x_recv[0] = p1x_send[0]
    arrived(p1x_recv.at[1:nx], p1x_rs)
    p2x_send[...] = jnp.sum(p1x_recv[...].astype(f32), axis=0).reshape(n, r, TILE)
    along(1 - c, lambda i: p2x_copy(i).start())
    lone_recv[spot(1 - c)] = lone_send[spot(1 - c)]
    arrived(lone_recv.at[0 : n - 1], lone_rs)
    lone = jnp.sum(lone_recv[...].astype(f32), axis=0).reshape(nx, r, TILE)
    p2_send[:, 1] = jnp.concatenate([lone, lone], axis=1).astype(bf16)
    pair_recv[spot(c)] = pair_send[spot(c)]
    arrived(pair_recv.at[0 : n - 1], pair_rs)
    pair = [jnp.sum(pair_recv[:, k].astype(f32), axis=0).reshape(nx, r, TILE) for k in (0, 1)]
    p2_send[:, 0] = jnp.concatenate(pair, axis=1).astype(bf16)
    for slot in reversed(range(1, nx)):
        p2_copy(slot).start()
    left(p1x_send.at[1:nx], p1x_ss)
    left(pair_send.at[0 : n - 1], pair_ss)
    left(lone_send.at[0 : n - 1], lone_ss)
    p2x_recv[spot(1 - c)] = p2x_send[spot(1 - c)]
    arrived(p2x_recv.at[0 : n - 1], p2x_rs)
    group0 = jnp.sum(p2x_recv[...], axis=0)
    p2_recv[0] = p2_send[0]
    arrived(p2_recv.at[1:nx], p2_rs)
    sums = jnp.sum(p2_recv[...].astype(f32), axis=0)
    groups = sums[0, :r], sums[0, r:], sums[1, :r]

    cuts = (1 - c, c)
    pairs = ((group0, groups[2]), (groups[0], groups[1]))
    for q in (0, 1):
        p3_send[q] = jnp.concatenate(pairs[q], axis=0).astype(bf16)

    def p3_copy(q, i):
        axis = 1 - cuts[q]
        return remote(p3_send.at[q], p3_recv.at[q, spot(axis)], p3_ss.at[q], p3_rs.at[q], (to(axis, i), feat))

    for off in around(n):
        for q in (0, 1):
            p3_copy(q, lax.rem(spot(1 - cuts[q]) + off, n)).start()
    left(p2x_send.at[0 : n - 1], p2x_ss)
    left(p2_send.at[1:nx], p2_ss)
    for q in (0, 1):
        p3_recv[q, spot(1 - cuts[q])] = p3_send[q]
        arrived(p3_recv.at[q, 0 : n - 1], p3_rs.at[q])
        res[q] = jnp.sum(p3_recv[q].astype(f32), axis=0).reshape(2, r, TILE)

    def p4_copy(q, i):
        return remote(res.at[q], wg_acc.at[spot(cuts[q]), q], p4_ss.at[q], p4_rs.at[q], (to(cuts[q], i), feat))

    for off in around(n):
        for q in (0, 1):
            p4_copy(q, lax.rem(spot(cuts[q]) + off, n)).start()
    for q in (0, 1):
        wg_acc[spot(cuts[q]), q] = res[q]
    for q in (0, 1):
        left(p3_recv.at[q, 0 : n - 1], p3_ss.at[q])
    for q in (0, 1):
        left(wg_acc.at[0 : n - 1, q], p4_ss.at[q])
    for q in (0, 1):
        arrived(wg_acc.at[0 : n - 1, q], p4_rs.at[q])
        for i in range(n):
            for k in (0, 1):
                block = 2 * q + k
                wg_out[i * r : (i + 1) * r, block * TILE : (block + 1) * TILE] = wg_acc[i, q, k]


def solution(mesh):
    nx = mesh.shape["feat"] // 2
    n = round(mesh.shape["dp"] ** 0.5)

    def shards(source_feat, weight, tile_index, tile_count, tile_mask, cotangent):
        nblk, maxt, tile, _ = tile_mask.shape
        width = source_feat.shape[1]
        hid = weight.shape[1]
        rows = TILE // n
        half = n // 2
        bf16, f32 = jnp.bfloat16, jnp.float32
        dma = lambda *shape: pltpu.SemaphoreType.DMA(shape)
        vm = pltpu.VMEM
        hbm = pl.BlockSpec(memory_space=pltpu.HBM)
        vmem = pl.BlockSpec(memory_space=pltpu.VMEM)
        hidden, weight_grad = pl.pallas_call(
            functools.partial(kernel, nx, n, maxt, width),
            out_shape=(
                vm((tile, hid), bf16),
                vm((width, hid), f32),
            ),
            in_specs=[hbm] * 6,
            out_specs=(vmem, vmem),
            scratch_shapes=[
                pltpu.SMEM((maxt, nblk), jnp.int32),
                pltpu.SMEM((1, nblk), jnp.int32),
                vm((width, source_feat.shape[0]), bf16),
                vm((source_feat.shape[0] // tile, width + 16, tile), bf16),
                vm((nx, 2, maxt, tile, tile), jnp.int32),
                vm((half, rows, hid), bf16),
                vm((2, tile, hid), bf16),
                vm((min(3, nx), half, rows, hid), bf16),
                vm((2, nx, n, rows, TILE), bf16),
                vm((nx, width, 2 * tile), bf16),
                vm((nx, width, 2 * tile), bf16),
                vm((2 * tile, hid), bf16),
                vm((2 * tile, hid), bf16),
                vm((nx, TILE // 2, TILE), bf16),
                vm((nx, TILE // 2, TILE), bf16),
                vm((n, 2, nx // 2, rows, TILE), bf16),
                vm((n, 2, nx // 2, rows, TILE), bf16),
                vm((n, nx // 2, rows, TILE), bf16),
                vm((n, nx // 2, rows, TILE), bf16),
                vm((n, rows // 2, TILE), f32),
                vm((n, rows // 2, TILE), f32),
                vm((nx, 2, rows, TILE), bf16),
                vm((nx, 2, rows, TILE), bf16),
                vm((2, rows, TILE), bf16),
                vm((2, n, rows, TILE), bf16),
                vm((2, 2, rows // 2, TILE), f32),
                vm((n, 2, 2, rows // 2, TILE), f32),
                dma(2), dma(), dma(nx), dma(), dma(),
                dma(), dma(),
                dma(), dma(),
                dma(2), dma(2, 2),
                dma(2, 2), dma(2, 2),
                dma(), dma(),
                dma(), dma(),
                dma(), dma(),
                dma(), dma(),
                dma(), dma(),
                dma(), dma(),
                dma(), dma(),
                dma(2), dma(2),
                dma(2), dma(2),
            ],
            compiler_params=pltpu.CompilerParams(
                collective_id=0, has_side_effects=True, vmem_limit_bytes=40 * 1024 * 1024
            ),
        )(
            *(
                pltpu.with_memory_space_constraint(a, pltpu.HBM)
                for a in (
                    tile_index.T,
                    tile_count.reshape(1, nblk),
                    source_feat.T,
                    weight.reshape(half, rows, hid),
                    tile_mask,
                    cotangent,
                )
            )
        )
        return hidden, weight_grad

    in_specs = (
        P("dp", "feat"),
        P("feat", None),
        P("dp", None),
        P("dp"),
        P("dp", None, None, None),
        P(("dp", "feat"), None),
    )
    out_specs = (P(("dp", "feat"), None), P("feat", None))
    return jax.shard_map(shards, mesh=mesh, in_specs=in_specs, out_specs=out_specs, check_vma=False)
```
